256 devices in a mesh: cube: 32 (over y, z_lo, x), col: 8 (over z_hi, core).
Axes of the slice: x: 4, y: 4, z: 8 (z_hi: 4, z_lo: 2; z = z_hi * 2 + z_lo), core: 2. Of those that a mesh axis runs over, the one named last changes fastest.
Arguments:
- ginv: float32 [8192, 8192], P('cube'), may hold values from -6 to 6
- ufactor: float32 [2, 4096, 2048], P(None, 'cube', 'col'), may hold values from -0.09375 to 0.09375
- dinv: float32 [2, 2048], P(None, 'col'), may hold values from 0.5 to 2
- tile_map: int32 [2, 16], replicated, may hold values from 0 to 31, as said below
- counts: int32 [2], replicated, may hold values from 1 to 4096, as said below
- assign: int32 [2], replicated, may hold values from 0 to 1, each once
Outputs:
- cross: float32 [2, 8192, 2048], P(None, 'cube', 'col')
- resist: float32 [2, 8192, 2048], P(None, 'cube', 'col')
- sigma_ff: float32 [2048, 2, 2048], P('cube', None, 'col')
The draws below stay inside these ranges and needn't reach their ends.
Inputs may be any that keep to these rules, and one draw needn't show every extreme that they name: `tile_map`: the two rows together hold every tile 0 to 31 exactly once. `counts`: one of the two fronts has all 4096 rows live.
All inputs are finite; a program needn't handle non-finite values.
Results may differ from the reference program's by a relative error of at most 0.0001.
Values sent between devices are 32-bit elements; how exact they have to be, the bound alone decides.
No kernel may reach another device: no remote copies, remote signals or barrier semaphores. Data moves between devices by JAX's collectives and lax.ppermute only.
A program may use at most 128 MiB of HBM per device.

```python
import math
import jax
import jax.numpy as jnp
from jax import lax

TILE = 256
P_SIZE = 2048
NF = 2
MT = 32
M = 8192
KS = 4096


def draw_tile_map(key, part):
    order = jax.random.permutation(jax.random.fold_in(key, 11), MT)
    return order.reshape(2, MT // 2).astype(jnp.int32)


def draw_counts(key, part):
    key = jax.random.fold_in(key, 23)
    short = jax.random.randint(jax.random.fold_in(key, 41), (), 1, KS + 1).astype(jnp.int32)
    flip = jax.random.randint(jax.random.fold_in(key, 59), (), 0, 2).astype(jnp.int32)
    full = jnp.int32(KS)
    first = jnp.where(flip == 0, full, short)
    second = jnp.where(flip == 0, short, full)
    return jnp.stack([first, second]).astype(jnp.int32)


def level_of(own_key, extent, pieces, low, high):
    loudness, own = 1.0, jax.random.fold_in(own_key, 6)
    for position, parts in pieces:
        steps = jnp.exp(jax.random.uniform(jax.random.fold_in(own, position), (parts,), jnp.float32, low / len(pieces), high / len(pieces)))
        loudness = loudness * jnp.repeat(steps, extent[position] // parts).reshape([-1 if axis == position else 1 for axis in range(len(extent))])
    return loudness


def scatter_about(own_key, shape, deviation, bound, shards=(), kind=jnp.bfloat16):
    factor_of = level_of(own_key, shape, shards, -0.22, 0.18) if shards else 1.0
    values = jax.random.normal(own_key, shape, jnp.float32) * deviation * factor_of
    return jnp.minimum(jnp.maximum(values, -bound), bound).astype(kind)


def setup_inputs(seed: int = 0) -> dict:
    seeds = jax.random.split(jax.random.key(seed), 7)
    ginv = scatter_about(seeds[0], (M, M), 1.0, 6.0, ((0, 32),), jnp.float32)
    ufactor = scatter_about(seeds[1], (NF, KS, P_SIZE), KS ** -0.5, 0.09375, ((1, 32), (2, 8)), jnp.float32)
    dinv = jnp.clip(jnp.exp(math.log(2.0) - 1.3862944 * jax.random.uniform(seeds[2], (NF, P_SIZE), jnp.float32) ** level_of(seeds[2], (NF, P_SIZE), ((1, 8),), -0.2, 0.2)), 0.5, 2.0)
    tile_map = draw_tile_map(jax.random.fold_in(seeds[6], 71), 0)
    counts = draw_counts(jax.random.fold_in(seeds[6], 71), 0)
    assign = jax.random.permutation(seeds[5], NF).astype(jnp.int32)
    return dict(ginv=ginv, ufactor=ufactor, dinv=dinv, tile_map=tile_map, counts=counts, assign=assign)


def reference(ginv, ufactor, dinv, tile_map, counts, assign):
    highest = lax.Precision.HIGHEST
    order = ginv.shape[0]
    tiles = order // TILE
    k_tiles = tile_map.shape[1]
    sep_rows = k_tiles * TILE
    gdiag = jnp.diagonal(ginv)
    gcols = ginv.reshape(order, tiles, TILE)
    crosses = []
    resists = []
    sigmas = []
    for front in range(2):
        u_front = jnp.take(ufactor, assign[front], axis=0)
        d_front = jnp.take(dinv, assign[front], axis=0)
        live_rows = (jnp.arange(sep_rows, dtype=jnp.int32) < counts[front]).astype(ginv.dtype)
        gsel = jnp.take(gcols, tile_map[front], axis=1).reshape(order, sep_rows) * live_rows[None, :]
        v_front = jnp.dot(gsel, u_front, precision=highest)
        v_rows = jnp.take(v_front.reshape(tiles, TILE, -1), tile_map[front], axis=0)
        v_rows = v_rows.reshape(sep_rows, -1)
        u_live = u_front * live_rows[:, None]
        sigma = jnp.dot(u_live.T, v_rows, precision=highest) + jnp.diag(d_front)
        row_live = jnp.zeros((tiles, TILE), ginv.dtype).at[tile_map[front]].set(live_rows.reshape(k_tiles, TILE))
        row_live = row_live.reshape(-1)
        resist = row_live[:, None] * (jnp.diagonal(sigma)[None, :] + gdiag[:, None] + 2.0 * v_front)
        crosses.append(-v_front)
        resists.append(resist)
        sigmas.append(sigma)
    return jnp.stack(crosses), jnp.stack(resists), jnp.stack(sigmas, axis=1)
```

```python
import functools

import jax
import jax.numpy as jnp
from jax import lax
from jax.experimental import pallas as pl
from jax.experimental.pallas import tpu as pltpu
from jax.sharding import PartitionSpec as P

AXES = ("cube", "col")
F32 = jnp.float32
VMEM = pltpu.VMEM
SMEM = pltpu.SMEM


def index_of(x, y, zl, zh, core):
    return ((y * 2 + zl) * 4 + x) * 8 + zh * 2 + core


def table(move):
    pairs = []
    for y in range(4):
        for zl in range(2):
            for x in range(4):
                for zh in range(4):
                    for core in range(2):
                        pairs.append(
                            (index_of(x, y, zl, zh, core), index_of(*move(x, y, zl, zh, core)))
                        )
    return pairs


def send_pq(v, dp, dq):
    def move(x, y, zl, zh, core):
        dx, dy = (dp, dq) if core == 0 else (dq, dp)
        return (x + dx) % 4, (y + dy) % 4, zl, zh, core

    return lax.ppermute(v, AXES, table(move))


def send_pair(v):
    return lax.ppermute(v, AXES, table(lambda x, y, zl, zh, core: (x, y, 1 - zl, zh, core)))


def send_core(v):
    return lax.ppermute(v, AXES, table(lambda x, y, zl, zh, core: (x, y, zl, zh, 1 - core)))


def send_zh(v, d):
    return lax.ppermute(v, AXES, table(lambda x, y, zl, zh, core: (x, y, zl, (zh + d) % 4, core)))


def split(a):
    hi = a.astype(jnp.bfloat16)
    lo = (a - hi.astype(F32)).astype(jnp.bfloat16)
    return hi, lo


def dot3(a, b, dims):
    ah, al = split(a)
    bh, bl = split(b)
    dg = functools.partial(lax.dot_general, dimension_numbers=(dims, ((), ())),
                           preferred_element_type=F32)
    return dg(ah, bh) + (dg(ah, bl) + dg(al, bh))


def v_kernel(first, cb, meta, g00, g01, g10, g11, u0, u1, *refs):
    if first:
        v_out, own_out = refs
    else:
        v_in, own_in, v_out, own_out = refs
    k = pl.program_id(0)

    @pl.when(k == 0)
    def _():
        if first:
            v_out[...] = jnp.zeros_like(v_out)
            own_out[...] = jnp.zeros_like(own_out)
        else:
            v_out[...] = v_in[...]
            own_out[...] = own_in[...]

    rows = lax.broadcasted_iota(jnp.int32, (128, 256), 0)
    gs = ((g00, g01), (g10, g11))
    us = (u0, u1)
    for s in range(2):
        parts = []
        for g in range(2):
            base = ((g * 4 + k) * 2 + s) * 2
            live = meta[base]
            half = meta[base + 1]
            u = jnp.where(rows < live, us[g][0, s], 0.0)
            parts.append(u)

            @pl.when(half >= 0)
            def _():
                own_out[pl.ds(pl.multiple_of(half * 128, 128), 128), :] = u

        uu = jnp.concatenate(parts, axis=0)
        gg = jnp.concatenate([gs[0][s][...], gs[1][s][...]], axis=1)
        v_out[s] += dot3(gg, uu, ((1,), (0,)))


def v_call(ginv, ua, ub, cb, meta, carry):
    def gspec(g, s):
        return pl.BlockSpec((256, 128), lambda k, cb, meta: (0, cb[(g * 4 + k) * 2 + s]))

    uspec = pl.BlockSpec((1, 2, 128, 256), lambda k, cb, meta: (k, 0, 0, 0))
    vspec = pl.BlockSpec((2, 256, 256), lambda k, cb, meta: (0, 0, 0))
    ospec = pl.BlockSpec((256, 256), lambda k, cb, meta: (0, 0))
    first = carry is None
    extra = [] if first else [vspec, ospec]
    aliases = {} if first else {8: 0, 9: 1}
    return pl.pallas_call(
        functools.partial(v_kernel, first),
        grid_spec=pltpu.PrefetchScalarGridSpec(
            num_scalar_prefetch=2,
            grid=(4,),
            in_specs=[gspec(0, 0), gspec(0, 1), gspec(1, 0), gspec(1, 1), uspec, uspec] + extra,
            out_specs=[vspec, ospec],
        ),
        out_shape=[jax.ShapeDtypeStruct((2, 256, 256), F32), jax.ShapeDtypeStruct((256, 256), F32)],
        input_output_aliases=aliases,
        compiler_params=pltpu.CompilerParams(vmem_limit_bytes=24 * 2**20),
        cost_estimate=pl.CostEstimate(flops=3 * 2 * 256 * 2048 * 256, bytes_accessed=6 * 2**20,
                                      transcendentals=0),
        name="v_part",
    )(cb, meta, ginv, ginv, ginv, ginv, ua, ub, *(() if first else carry))


def prod_kernel(pos, v, own, c1, c2a, c2b, c3, o_own, o1, o2a, o2b, o3, m0, m1, m2, m3, whole):
    x, y, zh, core = pos[0], pos[1], pos[2], pos[3]
    vv = v[0]
    vh, vl = split(vv)

    def dg(a, b):
        return lax.dot_general(a, b, (((0,), (0,)), ((), ())), preferred_element_type=F32)

    mine = own[...]
    for k in range(4):
        for side in range(2):
            if k == 2:
                u = jnp.concatenate([(c2a, o2a)[side][...], (c2b, o2b)[side][...]], axis=0)
            else:
                u = ((own, o_own), (c1, o1), None, (c3, o3))[k][side][...]
            uh, ul = split(u)
            block = lax.rem(zh + 4 - k, 4) * 2 + (core if side == 0 else 1 - core)
            whole[block] = dg(uh, vh) + (dg(uh, vl) + dg(ul, vh))
    diag = jnp.sum(mine * vv, axis=0, keepdims=True)
    for k, m in enumerate((m0, m1, m2, m3)):
        for i in range(8):
            b = jnp.where(core == 0, i, 2 * lax.rem(y + k, 4) + i // 4)
            sub = jnp.where(core == 0, lax.rem(x + k, 4), i % 4)
            m[i * 64:(i + 1) * 64, :] = whole[b, pl.ds(pl.multiple_of(sub * 64, 64), 64), :]
        m[512:520, :] = jnp.broadcast_to(diag, (8, 256))


def prod_call(pos, v, pieces):
    full = lambda shape: pl.BlockSpec(shape, lambda i, pos: (0,) * len(shape))
    vspec = pl.BlockSpec((1, 256, 256), lambda i, pos: (pos[4], 0, 0))
    big, small, msg = full((256, 256)), full((128, 256)), full((520, 256))
    ins = [big, big, small, small, big]
    return pl.pallas_call(
        prod_kernel,
        grid_spec=pltpu.PrefetchScalarGridSpec(
            num_scalar_prefetch=1, grid=(1,),
            in_specs=[vspec] + ins + ins, out_specs=[msg] * 4,
            scratch_shapes=[VMEM((8, 256, 256), F32)],
        ),
        out_shape=[jax.ShapeDtypeStruct((520, 256), F32)] * 4,
        compiler_params=pltpu.CompilerParams(vmem_limit_bytes=24 * 2**20),
        name="product",
    )(pos, v, *pieces)


def sum1_kernel(pos, r0, r1, r2, r3, m0, m1, m2, m3):
    x, y, zl, core = pos[0], pos[1], pos[2], pos[3]
    rs = (r0, r1, r2, r3)

    def both(rows):
        vals = [r[rows, :] for r in rs]
        out = []
        for s in range(2):
            total = None
            for k in range(4):
                term = jnp.where(pos[4 + k] == s, vals[k], 0.0)
                total = term if total is None else total + term
            out.append(total)
        return out

    d = both(pl.ds(512, 8))
    for k, m in enumerate((m0, m1, m2, m3)):
        for zrel in range(2):
            zb = lax.rem(zl + zrel, 2)
            at = jnp.where(core == 0, 2 * lax.rem(y + k, 4) + zb, zb * 4 + lax.rem(x + k, 4))
            pair = both(pl.ds(pl.multiple_of(at * 64, 64), 64))
            for s in range(2):
                m[(zrel * 2 + s) * 64:(zrel * 2 + s + 1) * 64, :] = pair[s]
        m[256:264, :] = d[0]
        m[264:272, :] = d[1]


def sum1_call(pos, rs):
    spec = pl.BlockSpec(memory_space=VMEM)
    return pl.pallas_call(
        sum1_kernel,
        in_specs=[pl.BlockSpec(memory_space=SMEM)] + [spec] * 4,
        out_specs=[spec] * 4,
        out_shape=[jax.ShapeDtypeStruct((272, 256), F32)] * 4,
        compiler_params=pltpu.CompilerParams(vmem_limit_bytes=16 * 2**20),
        name="sum_first",
    )(pos, *rs)


def sum2_kernel(r0, r1, r2, r3, keep, away):
    for rows, o, to in ((0, keep, 0), (128, away, 0)):
        o[to:to + 128, :] = (r0[rows:rows + 128, :] + r1[rows:rows + 128, :]) + (
            r2[rows:rows + 128, :] + r3[rows:rows + 128, :])
    d = (r0[256:272, :] + r1[256:272, :]) + (r2[256:272, :] + r3[256:272, :])
    keep[128:144, :] = d
    away[128:144, :] = d


def sum2_call(rs):
    spec = pl.BlockSpec(memory_space=VMEM)
    return pl.pallas_call(
        sum2_kernel,
        in_specs=[spec] * 4,
        out_specs=[spec] * 2,
        out_shape=[jax.ShapeDtypeStruct((144, 256), F32)] * 2,
        compiler_params=pltpu.CompilerParams(vmem_limit_bytes=16 * 2**20),
        name="sum_second",
    )(*rs)


def body(ginv, ufactor, dinv, tile_map, counts, assign):
    me = lax.axis_index("cube")
    col = lax.axis_index("col")
    x, zl, y = lax.rem(me, 4), lax.rem(me // 4, 2), me // 8
    zh, core = col // 2, lax.rem(col, 2)

    flip = assign[0] != 0
    tile_s = jnp.where(flip, tile_map[::-1], tile_map)
    counts_s = jnp.where(flip, counts[::-1], counts)

    step = jnp.arange(4, dtype=jnp.int32)
    plane = jnp.arange(2, dtype=jnp.int32)
    dp, dq = step[None, None, :], step[None, :, None]
    dx = jnp.where(core == 0, dp, dq)
    dy = jnp.where(core == 0, dq, dp)
    src = (((y + 4 - dy) % 4) * 2 + (zl + plane[:, None, None]) % 2) * 4 + (x + 4 - dx) % 4
    src = src[..., None]
    s_ids = plane[None, None, None, :]
    slot_tile = tile_s.reshape(-1)[s_ids * 16 + src // 2]
    cb = (slot_tile * 2 + src % 2).astype(jnp.int32)
    live = jnp.clip(counts_s[s_ids] - src * 128, 0, 128).astype(jnp.int32)
    half = jnp.where(slot_tile == me, src % 2, -1).astype(jnp.int32)
    meta = jnp.stack([live, half], axis=-1)

    in_one = jnp.any(tile_s[1][:, None] == jnp.arange(32, dtype=jnp.int32)[None, :], axis=0)
    front_of = in_one.astype(jnp.int32)
    s_own = front_of[me]

    a0 = ufactor
    b0 = send_pair(a0)
    a = [a0, send_pq(a0, 1, 0), send_pq(a0, 2, 0), send_pq(a0, -1, 0)]
    ga = jnp.stack(a)
    ga1 = send_pq(ga, 0, 1)
    ga3 = send_pq(ga, 0, -1)
    b = [b0, send_pq(b0, 1, 0), send_pq(b0, 2, 0), send_pq(b0, -1, 0)]
    gb = jnp.stack(b)
    gb1 = send_pq(gb, 0, 1)
    gb3 = send_pq(gb, 0, -1)
    ga2 = send_pq(ga1, 0, 1)
    gb2 = send_pq(gb3, 0, -1)

    def args(first, second):
        pick = lambda t: jnp.concatenate([t[first].reshape(-1), t[second].reshape(-1)])
        return pick(cb), pick(meta)

    carry = v_call(ginv, ga, gb, *args((0, 0), (1, 0)), None)
    carry = v_call(ginv, ga1, ga3, *args((0, 1), (0, 3)), carry)
    carry = v_call(ginv, gb1, gb3, *args((1, 1), (1, 3)), carry)
    v, own = v_call(ginv, ga2, gb2, *args((0, 2), (1, 2)), carry)

    c1 = send_zh(own, 1)
    c3 = send_zh(own, -1)
    c2a = send_zh(c1[:128], 1)
    c2b = send_zh(c3[128:], -1)
    near = [own, c1, c2a, c2b, c3]
    far = [send_core(t) for t in near]

    pos = jnp.stack([x, y, zh, core, s_own]).astype(jnp.int32)
    m = prod_call(pos, v, near + far)
    r = [m[0], send_pq(m[1], 1, 0), send_pq(m[2], 2, 0), send_pq(m[3], -1, 0)]
    from_p = jnp.where(core == 0, (y * 2 + zl) * 4 + (x + 4 - step) % 4,
                       (((y + 4 - step) % 4) * 2 + zl) * 4 + x)
    pos1 = jnp.concatenate([jnp.stack([x, y, zl, core]), front_of[from_p]]).astype(jnp.int32)
    m = sum1_call(pos1, r)
    r = [m[0], send_pq(m[1], 0, 1), send_pq(m[2], 0, 2), send_pq(m[3], 0, -1)]
    keep, away = sum2_call(r)
    total = keep + send_pair(away)

    front_order = lambda t: jnp.where(flip, t[::-1], t)
    d_local = front_order(dinv)
    sigma = front_order(total[:128].reshape(2, 64, 256)).transpose(1, 0, 2)
    rows = me * 64 + jnp.arange(64, dtype=jnp.int32)
    cols = col * 256 + jnp.arange(256, dtype=jnp.int32)
    on_diag = rows[:, None] == cols[None, :]
    sigma = sigma + jnp.where(on_diag[:, None, :], d_local[None], 0.0)
    diag = front_order(jnp.stack([total[128], total[136]])) + d_local

    block = lax.dynamic_slice_in_dim(ginv, me * 256, 256, 1)
    eye = jnp.arange(256)[:, None] == jnp.arange(256)[None, :]
    g_diag = jnp.sum(jnp.where(eye, block, 0.0), axis=1)
    slots = jnp.arange(16, dtype=jnp.int32)
    at = jnp.sum(jnp.where(tile_map == me, slots[None, :] + 1, 0), axis=1)
    row = (at[:, None] - 1) * 256 + jnp.arange(256, dtype=jnp.int32)[None, :]
    live_row = (at[:, None] > 0) & (row < counts[:, None])
    vf = front_order(v)
    cross = -vf
    resist = jnp.where(live_row[:, :, None], diag[:, None, :] + g_diag[None, :, None] + 2.0 * vf, 0.0)
    return cross, resist, sigma


def solution(mesh):
    in_specs = (P("cube", None), P(None, "cube", "col"), P(None, "col"), P(), P(), P())
    out_specs = (P(None, "cube", "col"), P(None, "cube", "col"), P("cube", None, "col"))
    return jax.shard_map(body, mesh=mesh, in_specs=in_specs, out_specs=out_specs, check_vma=False)
```

```python
import functools

import jax
import jax.numpy as jnp
from jax import lax
from jax.experimental import pallas as pl
from jax.experimental.pallas import tpu as pltpu
from jax.sharding import PartitionSpec as P

AXES = ("cube", "col")
F32 = jnp.float32
VMEM = pltpu.VMEM
SMEM = pltpu.SMEM


def index_of(x, y, zl, zh, core):
    return ((y * 2 + zl) * 4 + x) * 8 + zh * 2 + core


def table(move):
    pairs = []
    for y in range(4):
        for zl in range(2):
            for x in range(4):
                for zh in range(4):
                    for core in range(2):
                        pairs.append(
                            (index_of(x, y, zl, zh, core), index_of(*move(x, y, zl, zh, core)))
                        )
    return pairs


def send_pq(v, dp, dq):
    def move(x, y, zl, zh, core):
        dx, dy = (dp, dq) if core == 0 else (dq, dp)
        return (x + dx) % 4, (y + dy) % 4, zl, zh, core

    return lax.ppermute(v, AXES, table(move))


def send_x(v, d):
    return lax.ppermute(v, AXES, table(lambda x, y, zl, zh, core: ((x + d) % 4, y, zl, zh, core)))


def send_y(v, d):
    return lax.ppermute(v, AXES, table(lambda x, y, zl, zh, core: (x, (y + d) % 4, zl, zh, core)))


def send_pair(v):
    return lax.ppermute(v, AXES, table(lambda x, y, zl, zh, core: (x, y, 1 - zl, zh, core)))


def send_core(v):
    return lax.ppermute(v, AXES, table(lambda x, y, zl, zh, core: (x, y, zl, zh, 1 - core)))


def send_zh(v, d):
    return lax.ppermute(v, AXES, table(lambda x, y, zl, zh, core: (x, y, zl, (zh + d) % 4, core)))


def split(a):
    hi = a.astype(jnp.bfloat16)
    lo = (a - hi.astype(F32)).astype(jnp.bfloat16)
    return hi, lo


def dot3(a, b, dims):
    ah, al = split(a)
    bh, bl = split(b)
    dg = functools.partial(lax.dot_general, dimension_numbers=(dims, ((), ())),
                           preferred_element_type=F32)
    return dg(ah, bh) + (dg(ah, bl) + dg(al, bh))


def v_kernel(first, last, n, sizes, cb, meta, *refs):
    gs, refs = refs[:2 * n], refs[2 * n:]
    us, refs = refs[:len(sizes)], refs[len(sizes):]
    if not first:
        (v_in, own_in, ut_in), refs = refs[:3], refs[3:]
    v_out, own_out, ut_out = refs[:3]
    turned = refs[-1]
    if first:
        v_out[...] = jnp.zeros_like(v_out)
        own_out[...] = jnp.zeros_like(own_out)
        ut_out[...] = jnp.zeros_like(ut_out)
    else:
        v_out[...] = v_in[...]
        own_out[...] = own_in[...]
        ut_out[...] = ut_in[...]
    sub = meta[8 * n]
    rows = lax.broadcasted_iota(jnp.int32, (128, 256), 0)
    where = [(u, k) for u, size in zip(us, sizes) for k in range(size)]
    for s in range(2):
        parts = []
        for b, (u, k) in enumerate(where):
            base = (b * 2 + s) * 4
            part = jnp.where(rows < meta[base], u[k, s], 0.0)
            parts.append(part)

            @pl.when(meta[base + 1] >= 0)
            def _():
                at = pl.multiple_of(meta[base + 1] * 128, 128)
                own_out[pl.ds(at, 128), :] = part

            @pl.when(meta[base + 2] >= 0)
            def _():
                turned[...] = part.T
                ut_out[meta[base + 2]] = turned[pl.ds(pl.multiple_of(sub * 64, 64), 64), :]

        uu = jnp.concatenate(parts, axis=0)
        gg = jnp.concatenate([gs[b * 2 + s][...] for b in range(n)], axis=1)
        v_out[s] += dot3(gg, uu, ((1,), (0,)))
    if last:
        msg = refs[3]
        v_own = v_out[meta[8 * n + 1]]
        msg[:256, :] = v_own
        diag = jnp.sum(own_out[...] * v_own, axis=0, keepdims=True)
        msg[256:264, :] = jnp.broadcast_to(diag, (8, 256))


def v_call(ginv, us, cb, meta, carry, last=False):
    sizes = tuple(u.shape[0] for u in us)
    n = sum(sizes)

    def gspec(i):
        return pl.BlockSpec((256, 128), lambda _, cb, meta: (0, cb[i]))

    def full(*shape):
        return pl.BlockSpec(shape, lambda _, cb, meta: (0,) * len(shape))

    first = carry is None
    shapes = [(2, 256, 256), (256, 256), (8, 64, 128)]
    extra = [] if first else [full(*shape) for shape in shapes]
    at = 2 + 2 * n + len(us)
    aliases = {} if first else {at + i: i for i in range(3)}
    if last:
        shapes.append((264, 256))
    return pl.pallas_call(
        functools.partial(v_kernel, first, last, n, sizes),
        grid_spec=pltpu.PrefetchScalarGridSpec(
            num_scalar_prefetch=2,
            grid=(1,),
            in_specs=[gspec(i) for i in range(2 * n)] + [full(z, 2, 128, 256) for z in sizes] + extra,
            out_specs=[full(*shape) for shape in shapes],
            scratch_shapes=[VMEM((256, 128), F32)],
        ),
        out_shape=[jax.ShapeDtypeStruct(shape, F32) for shape in shapes],
        input_output_aliases=aliases,
        compiler_params=pltpu.CompilerParams(vmem_limit_bytes=57 * 2**20),
        cost_estimate=pl.CostEstimate(flops=3 * 4 * 256 * 128 * n * 256,
                                      bytes_accessed=(n + 3) * 2**19, transcendentals=0),
        name="v_part",
    )(cb, meta, *([ginv] * (2 * n)), *us, *(() if first else carry))


def prod_kernel(pos, v0, v1, v2, v3, n0, n1, n2a, n2b, n3, f0, f1, f2a, f2b, f3,
                m0, m1, m2, m3, acc):
    x, y, zl, zh, core = pos[0], pos[1], pos[2], pos[3], pos[4]
    acc[...] = jnp.zeros_like(acc)
    vs = (v0, v1, v2, v3)
    us = ((n0, f0), (n1, f1), ((n2a, n2b), (f2a, f2b)), (n3, f3))
    order = [(k, side) for k in range(4) for side in range(2)]
    for t in range(4):
        tile = lax.rem(x + 4 - t, 4)
        left = []
        for k, side in order:
            if k == 2:
                lo, hi = us[k][side]
                at = lax.rem(tile, 2) * 2
                pair = [jnp.where(tile < 2, lo[at + h], hi[at + h]) for h in range(2)]
            else:
                pair = [us[k][side][tile * 2 + h] for h in range(2)]
            left.append(jnp.concatenate(pair, axis=1))
        part = dot3(jnp.concatenate(left, axis=0), vs[t][:256, :], ((1,), (0,)))
        s = pos[5 + t]
        for i, (k, side) in enumerate(order):
            block = lax.rem(zh + 4 - k, 4) * 2 + (core if side == 0 else 1 - core)
            acc[s, block] += part[i * 64:(i + 1) * 64, :]
    diag = []
    for s in range(2):
        total = None
        for t in range(4):
            term = jnp.where(pos[5 + t] == s, vs[t][256:264, :], 0.0)
            total = term if total is None else total + term
        diag.append(total)
    for k, m in enumerate((m0, m1, m2, m3)):
        for zrel in range(2):
            for s in range(2):
                block = 2 * lax.rem(y + k, 4) + lax.rem(zl + zrel, 2)
                at = (zrel * 2 + s) * 64
                m[at:at + 64, :] = acc[s, block]
        m[256:264, :] = diag[0]
        m[264:272, :] = diag[1]


def prod_call(pos, vs, pieces):
    spec = pl.BlockSpec(memory_space=VMEM)
    return pl.pallas_call(
        prod_kernel,
        in_specs=[pl.BlockSpec(memory_space=SMEM)] + [spec] * 14,
        out_specs=[spec] * 4,
        out_shape=[jax.ShapeDtypeStruct((272, 256), F32)] * 4,
        scratch_shapes=[VMEM((2, 8, 64, 256), F32)],
        compiler_params=pltpu.CompilerParams(vmem_limit_bytes=24 * 2**20),
        cost_estimate=pl.CostEstimate(flops=3 * 2 * 512 * 1024 * 256, bytes_accessed=5 * 2**20,
                                      transcendentals=0),
        name="product",
    )(pos, *vs, *pieces)


def sum2_kernel(r0, r1, r2, r3, keep, away):
    for rows, o, to in ((0, keep, 0), (128, away, 0)):
        o[to:to + 128, :] = (r0[rows:rows + 128, :] + r1[rows:rows + 128, :]) + (
            r2[rows:rows + 128, :] + r3[rows:rows + 128, :])
    d = (r0[256:272, :] + r1[256:272, :]) + (r2[256:272, :] + r3[256:272, :])
    keep[128:144, :] = d
    away[128:144, :] = d


def sum2_call(rs):
    spec = pl.BlockSpec(memory_space=VMEM)
    return pl.pallas_call(
        sum2_kernel,
        in_specs=[spec] * 4,
        out_specs=[spec] * 2,
        out_shape=[jax.ShapeDtypeStruct((144, 256), F32)] * 2,
        compiler_params=pltpu.CompilerParams(vmem_limit_bytes=16 * 2**20),
        name="sum_second",
    )(*rs)


def body(ginv, ufactor, dinv, tile_map, counts, assign):
    me = lax.axis_index("cube")
    col = lax.axis_index("col")
    x, zl, y = lax.rem(me, 4), lax.rem(me // 4, 2), me // 8
    zh, core = col // 2, lax.rem(col, 2)

    flip = assign[0] != 0
    tile_s = jnp.where(flip, tile_map[::-1], tile_map)
    counts_s = jnp.where(flip, counts[::-1], counts)

    step = jnp.arange(4, dtype=jnp.int32)
    plane = jnp.arange(2, dtype=jnp.int32)
    dp, dq = step[None, None, :], step[None, :, None]
    dx = jnp.where(core == 0, dp, dq)
    dy = jnp.where(core == 0, dq, dp)
    src = (((y + 4 - dy) % 4) * 2 + (zl + plane[:, None, None]) % 2) * 4 + (x + 4 - dx) % 4
    src = src[..., None]
    s_ids = plane[None, None, None, :]
    slot_tile = tile_s.reshape(-1)[s_ids * 16 + src // 2]
    cb = (slot_tile * 2 + src % 2).astype(jnp.int32)
    live = jnp.clip(counts_s[s_ids] - src * 128, 0, 128).astype(jnp.int32)
    half = jnp.where(slot_tile == me, src % 2, -1).astype(jnp.int32)
    spot = slot_tile - (y * 2 + zl) * 4
    spot = jnp.where((spot >= 0) & (spot < 4), spot * 2 + src % 2, -1).astype(jnp.int32)
    meta = jnp.stack([live, half, spot, jnp.zeros_like(live)], axis=-1)

    in_one = jnp.any(tile_s[1][:, None] == jnp.arange(32, dtype=jnp.int32)[None, :], axis=0)
    front_of = in_one.astype(jnp.int32)
    s_own = front_of[me]

    pin = lax.optimization_barrier

    def part(*which):
        pick = lambda t: jnp.concatenate([t[g, q, lo:hi].reshape(-1) for g, q, lo, hi in which])
        return pick(cb), jnp.concatenate([pick(meta), jnp.stack([x, s_own]).astype(jnp.int32)])

    a0 = ufactor
    ga = jnp.stack([a0, send_pq(a0, 1, 0), send_pq(a0, 2, 0), send_pq(a0, -1, 0)])
    ga1 = send_pq(ga, 0, 1)
    ga3 = send_pq(ga, 0, -1)
    b1 = send_pair(ga[:2])
    b2 = send_pair(ga[2:])
    carry = v_call(ginv, [ga], *part((0, 0, 0, 4)), None)
    ga1, ga3, b1, carry = pin((ga1, ga3, b1, carry))
    ga2a = send_pq(ga1[:2], 0, 1)
    ga2b = send_pq(ga3[2:], 0, -1)
    b11 = send_pq(b1, 0, 1)
    b13 = send_pq(b1, 0, -1)
    carry = v_call(ginv, [ga1, ga3], *part((0, 1, 0, 4), (0, 3, 0, 4)), carry)
    b2, carry, ga2a, ga2b = pin((b2, carry, ga2a, ga2b))
    b21 = send_pq(b2, 0, 1)
    b23 = send_pq(b2, 0, -1)
    b11, b13, b2 = pin((b11, b13, b2))
    b12 = send_pq(b11, 0, 1)
    carry = v_call(ginv, [ga2a, ga2b, b1, b2],
                   *part((0, 2, 0, 2), (0, 2, 2, 4), (1, 0, 0, 2), (1, 0, 2, 4)), carry)
    b21, b23, carry = pin((b21, b23, carry))
    b22 = send_pq(b23, 0, -1)
    carry = v_call(ginv, [b11, b13, b21, b23],
                   *part((1, 1, 0, 2), (1, 3, 0, 2), (1, 1, 2, 4), (1, 3, 2, 4)), carry)
    b12, b22, carry = pin((b12, b22, carry))
    v, _, ut, msg = v_call(ginv, [b12, b22], *part((1, 2, 0, 2), (1, 2, 2, 4)), carry, True)

    c1 = send_zh(ut, 1)
    c3 = send_zh(ut, -1)
    vs = [msg, send_x(msg, 1), send_x(msg, 2), send_x(msg, -1)]
    c2a = send_zh(c1[:4], 1)
    c2b = send_zh(c3[4:], -1)
    near = [ut, c1, c2a, c2b, c3]
    far = [send_core(t) for t in near]

    fronts = front_of[(y * 2 + zl) * 4 + (x + 4 - step) % 4]
    pos = jnp.concatenate([jnp.stack([x, y, zl, zh, core]), fronts]).astype(jnp.int32)
    m = prod_call(pos, vs, near + far)
    r = [m[0], send_y(m[1], 1), send_y(m[2], 2), send_y(m[3], -1)]
    keep, away = sum2_call(r)
    total = keep + send_pair(away)

    front_order = lambda t: jnp.where(flip, t[::-1], t)
    d_local = front_order(dinv)
    sigma = front_order(total[:128].reshape(2, 64, 256)).transpose(1, 0, 2)
    rows = me * 64 + jnp.arange(64, dtype=jnp.int32)
    cols = col * 256 + jnp.arange(256, dtype=jnp.int32)
    on_diag = rows[:, None] == cols[None, :]
    sigma = sigma + jnp.where(on_diag[:, None, :], d_local[None], 0.0)
    diag = front_order(jnp.stack([total[128], total[136]])) + d_local

    block = lax.dynamic_slice_in_dim(ginv, me * 256, 256, 1)
    eye = jnp.arange(256)[:, None] == jnp.arange(256)[None, :]
    g_diag = jnp.sum(jnp.where(eye, block, 0.0), axis=1)
    slots = jnp.arange(16, dtype=jnp.int32)
    at = jnp.sum(jnp.where(tile_map == me, slots[None, :] + 1, 0), axis=1)
    row = (at[:, None] - 1) * 256 + jnp.arange(256, dtype=jnp.int32)[None, :]
    live_row = (at[:, None] > 0) & (row < counts[:, None])
    vf = front_order(v)
    cross = -vf
    resist = jnp.where(live_row[:, :, None], diag[:, None, :] + g_diag[None, :, None] + 2.0 * vf, 0.0)
    return cross, resist, sigma


def solution(mesh):
    in_specs = (P("cube", None), P(None, "cube", "col"), P(None, "col"), P(), P(), P())
    out_specs = (P(None, "cube", "col"), P(None, "cube", "col"), P("cube", None, "col"))
    return jax.shard_map(body, mesh=mesh, in_specs=in_specs, out_specs=out_specs, check_vma=False)
```

```python
import functools

import jax
import jax.numpy as jnp
from jax import lax
from jax.experimental import pallas as pl
from jax.experimental.pallas import tpu as pltpu
from jax.sharding import PartitionSpec as P

AXES = ("cube", "col")
F32 = jnp.float32
VMEM = pltpu.VMEM
SMEM = pltpu.SMEM
VLIM = 24
COST = 4


def index_of(x, y, zl, zh, core):
    return ((y * 2 + zl) * 4 + x) * 8 + zh * 2 + core


def table(move):
    pairs = []
    for y in range(4):
        for zl in range(2):
            for x in range(4):
                for zh in range(4):
                    for core in range(2):
                        pairs.append(
                            (index_of(x, y, zl, zh, core), index_of(*move(x, y, zl, zh, core)))
                        )
    return pairs


def send_pq(v, dp, dq):
    def move(x, y, zl, zh, core):
        dx, dy = (dp, dq) if core == 0 else (dq, dp)
        return (x + dx) % 4, (y + dy) % 4, zl, zh, core

    return lax.ppermute(v, AXES, table(move))


def send_x(v, d):
    return lax.ppermute(v, AXES, table(lambda x, y, zl, zh, core: ((x + d) % 4, y, zl, zh, core)))


def send_x_flip(v, bit):
    return lax.ppermute(v, AXES, table(lambda x, y, zl, zh, core: (x ^ bit, y, zl, zh, core)))


def send_y(v, d):
    return lax.ppermute(v, AXES, table(lambda x, y, zl, zh, core: (x, (y + d) % 4, zl, zh, core)))


def send_pair(v):
    return lax.ppermute(v, AXES, table(lambda x, y, zl, zh, core: (x, y, 1 - zl, zh, core)))


def send_core(v):
    return lax.ppermute(v, AXES, table(lambda x, y, zl, zh, core: (x, y, zl, zh, 1 - core)))


def send_zh(v, d):
    return lax.ppermute(v, AXES, table(lambda x, y, zl, zh, core: (x, y, zl, (zh + d) % 4, core)))


def split(a):
    hi = a.astype(jnp.bfloat16)
    lo = (a - hi.astype(F32)).astype(jnp.bfloat16)
    return hi, lo


def dot3(a, b, dims):
    ah, al = split(a)
    bh, bl = split(b)
    dg = functools.partial(lax.dot_general, dimension_numbers=(dims, ((), ())),
                           preferred_element_type=F32)
    return dg(ah, bh) + (dg(ah, bl) + dg(al, bh))


def plan_kernel(tile_map, counts, assign, cb, meta, info):
    me, col = lax.axis_index("cube"), lax.axis_index("col")
    x, zl, y = lax.rem(me, 4), lax.rem(lax.div(me, 4), 2), lax.div(me, 8)
    zh, core = lax.div(col, 2), lax.rem(col, 2)
    group = (y * 2 + zl) * 4
    flip = jnp.where(assign[0] != 0, 1, 0)
    for i, value in enumerate((x, y, zl, zh, core)):
        info[i] = value

    def fill(i, _):
        s, dp, dq, plane = i & 1, (i >> 1) & 3, (i >> 3) & 3, i >> 5
        dx = jnp.where(core == 0, dp, dq)
        dy = jnp.where(core == 0, dq, dp)
        src = (((y - dy) & 3) * 2 + ((zl + plane) & 1)) * 4 + ((x - dx) & 3)
        front = s ^ flip
        tile = tile_map[front, src >> 1]
        cb[i] = tile * 2 + (src & 1)
        live = jnp.clip(counts[front] - src * 128, 0, 128)
        meta[i] = live

        @pl.when((tile >= group) & (tile < group + 4))
        def _():
            piece = (tile - group) * 2 + (src & 1)
            meta[64 + piece] = i
            meta[72 + piece] = live

        return 0

    lax.fori_loop(0, 64, fill, 0)

    def look(i, _):
        front, j = i >> 4, i & 15
        tile = tile_map[front, j]

        @pl.when((tile >= group) & (tile < group + 4))
        def _():
            info[5 + ((x ^ tile) & 3)] = front ^ flip

        @pl.when(tile == me)
        def _():
            info[9] = front
            info[10] = jnp.clip(counts[front] - j * 256, 0, 256)

        return 0

    lax.fori_loop(0, 32, look, 0)
    info[11] = flip
    info[12] = me


def plan_call(tile_map, counts, assign):
    spec = pl.BlockSpec(memory_space=SMEM)
    return pl.pallas_call(
        plan_kernel,
        in_specs=[spec] * 3,
        out_specs=[spec] * 3,
        out_shape=[jax.ShapeDtypeStruct((size,), jnp.int32) for size in (64, 80, 16)],
        name="plan",
    )(tile_map, counts, assign)


def u_kernel(first, groups, meta, info, *refs):
    us, refs = refs[:len(groups)], refs[len(groups):]
    if not first:
        (own_in, ut_in), refs = refs[:2], refs[2:]
    own, ut, buf, turned, sem = refs

    def each(do):
        for piece in range(8):
            place = meta[64 + piece]
            for u, (base, size) in zip(us, groups):
                @pl.when((place >= base * 2) & (place < (base + size) * 2))
                def _():
                    at = place - base * 2
                    do(piece, pltpu.make_async_copy(u.at[at >> 1, at & 1], buf.at[piece],
                                                    sem.at[piece]))

    each(lambda piece, copy: copy.start())
    if first:
        own[...] = jnp.zeros_like(own)
        ut[...] = jnp.zeros_like(ut)
    else:
        own[...] = own_in[...]
        ut[...] = ut_in[...]
    x = info[0]
    rows = lax.broadcasted_iota(jnp.int32, (128, 256), 0)

    def take(piece, copy):
        copy.wait()
        part = jnp.where(rows < meta[72 + piece], buf[piece], 0.0)
        turned[...] = part.T
        ut[piece] = turned[pl.ds(pl.multiple_of(x * 64, 64), 64), :]

        @pl.when(x == piece // 2)
        def _():
            half = piece % 2
            own[half * 128:(half + 1) * 128, :] = part

    each(take)


def u_call(plan, us, starts, carry):
    groups = tuple((start, u.shape[0]) for start, u in zip(starts, us))
    first = carry is None
    smem, vmem, anywhere = (pl.BlockSpec(memory_space=m) for m in (SMEM, VMEM, pl.ANY))
    at = 2 + len(us)
    return pl.pallas_call(
        functools.partial(u_kernel, first, groups),
        in_specs=[smem] * 2 + [anywhere] * len(us) + ([] if first else [vmem] * 2),
        out_specs=[vmem] * 2,
        out_shape=[jax.ShapeDtypeStruct((256, 256), F32), jax.ShapeDtypeStruct((8, 64, 128), F32)],
        scratch_shapes=[VMEM((8, 128, 256), F32), VMEM((256, 128), F32),
                        pltpu.SemaphoreType.DMA((8,))],
        input_output_aliases={} if first else {at: 0, at + 1: 1},
        compiler_params=pltpu.CompilerParams(vmem_limit_bytes=16 * 2**20),
        name="u_rows",
    )(*plan[1:], *us, *(() if first else carry))


def v_kernel(first, last, groups, cb, meta, info, *refs):
    ginv, refs = refs[0], refs[1:]
    us, refs = refs[:len(groups)], refs[len(groups):]
    if not first:
        v_in, refs = refs[0], refs[1:]
    if last:
        own, refs = refs[0], refs[1:]
    v_out = refs[0]
    gbuf, ubuf, gsem, usem = refs[-4:]
    copies = []
    at = 0
    for i, (base, size) in enumerate(groups):
        mine = [pltpu.make_async_copy(us[i], ubuf.at[pl.ds(at, size)], usem.at[i])]
        for b in range(size):
            for s in range(2):
                column = pl.multiple_of(cb[(base + b) * 2 + s] * 128, 128)
                mine.append(pltpu.make_async_copy(
                    ginv.at[:, pl.ds(column, 128)],
                    gbuf.at[s, :, pl.ds((at + b) * 128, 128)],
                    gsem.at[(at + b) * 2 + s]))
        for c in mine:
            c.start()
        copies.append(mine)
        at += size
    rows = lax.broadcasted_iota(jnp.int32, (128, 256), 0)
    at = 0
    for i, (base, size) in enumerate(groups):
        for c in copies[i]:
            c.wait()
        for s in range(2):
            uu = jnp.concatenate(
                [jnp.where(rows < meta[(base + b) * 2 + s], ubuf[at + b, s], 0.0)
                 for b in range(size)], axis=0)
            gg = gbuf[s, :, at * 128:(at + size) * 128]
            part = dot3(gg, uu, ((1,), (0,)))
            if i > 0:
                part += v_out[s]
            elif not first:
                part += v_in[s]
            v_out[s] = part
        at += size
    if last:
        msg = refs[1]
        v_own = v_out[info[9] ^ info[11]]
        msg[:256, :] = v_own
        diag = jnp.sum(own[...] * v_own, axis=0, keepdims=True)
        msg[256:264, :] = jnp.broadcast_to(diag, (8, 256))


def v_call(ginv, plan, us, starts, carry, own=None):
    groups = tuple((start, u.shape[0]) for start, u in zip(starts, us))
    n = sum(size for _, size in groups)
    first, last = carry is None, own is not None
    shapes = [(2, 256, 256)]
    smem, vmem, anywhere = (pl.BlockSpec(memory_space=m) for m in (SMEM, VMEM, pl.ANY))
    extra = [t for t in (carry, own) if t is not None]
    if last:
        shapes.append((264, 256))
    out = pl.pallas_call(
        functools.partial(v_kernel, first, last, groups),
        in_specs=[smem] * 3 + [pl.BlockSpec(memory_space=pltpu.HBM)] + [anywhere] * len(us)
        + [vmem] * len(extra),
        out_specs=[vmem] * len(shapes),
        out_shape=[jax.ShapeDtypeStruct(shape, F32) for shape in shapes],
        scratch_shapes=[VMEM((2, 256, n * 128), F32), VMEM((n, 2, 128, 256), F32),
                        pltpu.SemaphoreType.DMA((2 * n,)), pltpu.SemaphoreType.DMA((len(us),))],
        compiler_params=pltpu.CompilerParams(vmem_limit_bytes=VLIM * 2**20),
        cost_estimate=pl.CostEstimate(flops=3 * 4 * 256 * 128 * n * 256,
                                      bytes_accessed=n * COST * 2**20, transcendentals=0),
        name="v_part",
    )(*plan, ginv, *us, *extra)
    return out if last else out[0]


def prod_kernel(pos, v0, v1, v2, v3, near, near2, far, far2, m0, m1, m2, m3, acc):
    x, y, zl, zh, core = pos[0], pos[1], pos[2], pos[3], pos[4]
    acc[...] = jnp.zeros_like(acc)
    vs = (v0, v1, v2, v3)
    order = [(k, side) for k in range(4) for side in range(2)]
    for t in range(4):
        tile = x ^ t
        left = []
        for k, side in order:
            u = (near2, far2)[side] if k == 2 else (near, far)[side].at[(0, 1, None, 2)[k]]
            left.append(jnp.concatenate([u[tile * 2 + h] for h in range(2)], axis=1))
        part = dot3(jnp.concatenate(left, axis=0), vs[t][:256, :], ((1,), (0,)))
        s = pos[5 + t]
        for i, (k, side) in enumerate(order):
            block = lax.rem(zh + 4 - k, 4) * 2 + (core if side == 0 else 1 - core)
            acc[s, block] += part[i * 64:(i + 1) * 64, :]
    diag = []
    for s in range(2):
        total = None
        for t in range(4):
            term = jnp.where(pos[5 + t] == s, vs[t][256:264, :], 0.0)
            total = term if total is None else total + term
        diag.append(total)
    for k, m in enumerate((m0, m1, m2, m3)):
        for zrel in range(2):
            for s in range(2):
                block = 2 * lax.rem(y + k, 4) + lax.rem(zl + zrel, 2)
                at = (zrel * 2 + s) * 64
                m[at:at + 64, :] = acc[s, block]
        m[256:264, :] = diag[0]
        m[264:272, :] = diag[1]


def prod_call(pos, vs, pieces):
    spec = pl.BlockSpec(memory_space=VMEM)
    return pl.pallas_call(
        prod_kernel,
        in_specs=[pl.BlockSpec(memory_space=SMEM)] + [spec] * 8,
        out_specs=[spec] * 4,
        out_shape=[jax.ShapeDtypeStruct((272, 256), F32)] * 4,
        scratch_shapes=[VMEM((2, 8, 64, 256), F32)],
        compiler_params=pltpu.CompilerParams(vmem_limit_bytes=24 * 2**20),
        cost_estimate=pl.CostEstimate(flops=3 * 2 * 512 * 1024 * 256, bytes_accessed=5 * 2**20,
                                      transcendentals=0),
        name="product",
    )(pos, *vs, *pieces)


def sum2_kernel(r0, r1, r2, r3, keep, away):
    for rows, o, to in ((0, keep, 0), (128, away, 0)):
        o[to:to + 128, :] = (r0[rows:rows + 128, :] + r1[rows:rows + 128, :]) + (
            r2[rows:rows + 128, :] + r3[rows:rows + 128, :])
    d = (r0[256:272, :] + r1[256:272, :]) + (r2[256:272, :] + r3[256:272, :])
    keep[128:144, :] = d
    away[128:144, :] = d


def sum2_call(rs):
    spec = pl.BlockSpec(memory_space=VMEM)
    return pl.pallas_call(
        sum2_kernel,
        in_specs=[spec] * 4,
        out_specs=[spec] * 2,
        out_shape=[jax.ShapeDtypeStruct((144, 256), F32)] * 2,
        compiler_params=pltpu.CompilerParams(vmem_limit_bytes=16 * 2**20),
        name="sum_second",
    )(*rs)


def cross_kernel(info, v, block, cross, base):
    flip = info[11]
    eye = lax.broadcasted_iota(jnp.int32, (256, 256), 0) == lax.broadcasted_iota(
        jnp.int32, (256, 256), 1)
    g_diag = jnp.sum(jnp.where(eye, block[...], 0.0), axis=1, keepdims=True)
    for f in range(2):
        vf = v[f ^ flip]
        cross[f] = -vf
        base[f] = g_diag + 2.0 * vf


def cross_call(info, v, ginv):
    full = pl.BlockSpec((2, 256, 256), lambda _, info: (0, 0, 0))
    return pl.pallas_call(
        cross_kernel,
        grid_spec=pltpu.PrefetchScalarGridSpec(
            num_scalar_prefetch=1, grid=(1,),
            in_specs=[full, pl.BlockSpec((256, 256), lambda _, info: (0, info[12]))],
            out_specs=[full, full],
        ),
        out_shape=[jax.ShapeDtypeStruct((2, 256, 256), F32)] * 2,
        name="cross",
    )(info, v, ginv)


def last_kernel(info, keep, came, dinv, base, resist, sigma):
    flip = info[11]
    rows = lax.broadcasted_iota(jnp.int32, (256, 256), 0)
    at = lax.broadcasted_iota(jnp.int32, (64, 256), 0) + lax.rem(info[12], 4) * 64
    on_diag = at == lax.broadcasted_iota(jnp.int32, (64, 256), 1)
    on_diag = on_diag & (info[12] // 4 == info[3] * 2 + info[4])
    for f in range(2):
        s = f ^ flip
        d = dinv[pl.ds(s, 1), :]
        total = keep[pl.ds(pl.multiple_of(s * 64, 64), 64), :] + came[
            pl.ds(pl.multiple_of(s * 64, 64), 64), :]
        sigma[:, f, :] = total + jnp.where(on_diag, d, 0.0)
        deep = pl.ds(pl.multiple_of(128 + s * 8, 8), 8)
        diag = (keep[deep, :] + came[deep, :])[0:1, :] + d
        live = jnp.where(info[9] == f, info[10], 0)
        resist[f] = jnp.where(rows < live, diag + base[f], 0.0)


def last_call(info, keep, came, dinv, base):
    spec = pl.BlockSpec(memory_space=VMEM)
    return pl.pallas_call(
        last_kernel,
        in_specs=[pl.BlockSpec(memory_space=SMEM)] + [spec] * 4,
        out_specs=[spec] * 2,
        out_shape=[jax.ShapeDtypeStruct((2, 256, 256), F32), jax.ShapeDtypeStruct((64, 2, 256), F32)],
        name="last",
    )(info, keep, came, dinv, base)


def body(ginv, ufactor, dinv, tile_map, counts, assign):
    pin = lax.optimization_barrier

    a0 = ufactor
    b0 = send_pair(a0)
    ga = jnp.stack([a0, send_pq(a0, 1, 0), send_pq(a0, 2, 0), send_pq(a0, -1, 0)])
    ga, tile_map = pin((ga, tile_map))
    ga1 = send_pq(ga, 0, 1)
    ga3 = send_pq(ga, 0, -1)
    plan = plan_call(tile_map, counts, assign)
    info = plan[2]
    *b, plan = pin([b0, send_pq(b0, 1, 0), send_pq(b0, 2, 0), send_pq(b0, -1, 0), plan])
    gb = jnp.stack(b)
    gb1 = send_pq(gb, 0, 1)
    gb3 = send_pq(gb, 0, -1)
    carry = v_call(ginv, plan, [ga, gb], [0, 16], None)
    ga1, ga3, carry = pin((ga1, ga3, carry))
    ga2a = send_pq(ga1[:2], 0, 1)
    ga2b = send_pq(ga3[2:], 0, -1)
    carry = v_call(ginv, plan, [ga1, ga3], [4, 12], carry)
    gb1, gb3, carry = pin((gb1, gb3, carry))
    gb2a = send_pq(gb1[:2], 0, 1)
    gb2b = send_pq(gb3[2:], 0, -1)
    carry = v_call(ginv, plan, [gb1, gb3, ga2a, ga2b], [20, 28, 8, 10], carry)
    rows = u_call(plan, [ga, gb, ga1, ga3, gb1, gb3, ga2a, ga2b],
                  [0, 16, 4, 12, 20, 28, 8, 10], None)
    gb2a, gb2b, carry, rows = pin((gb2a, gb2b, carry, rows))
    own, ut = u_call(plan, [gb2a, gb2b], [24, 26], rows)

    c1, c3 = send_zh(ut, 1), send_zh(ut, -1)
    v, msg = v_call(ginv, plan, [gb2a, gb2b], [24, 26], carry, own)
    v1, v2 = send_x_flip(msg, 1), send_x_flip(msg, 2)
    c1, c3, ut, v1, v2 = pin((c1, c3, ut, v1, v2))
    vs = [msg, v1, v2, send_x_flip(v1, 2)]
    c2 = jnp.concatenate([send_zh(c1[:4], 1), send_zh(c3[4:], -1)])
    near = [jnp.stack([ut, c1, c3]), c2]
    far = [send_core(t) for t in near]
    cross, base = cross_call(info, v, ginv)

    m = prod_call(info, vs, near + far)
    r = [m[0], send_y(m[1], 1), send_y(m[2], 2), send_y(m[3], -1)]
    keep, away = sum2_call(r)
    came = send_pair(away)
    resist, sigma = last_call(info, keep, came, dinv, base)
    return cross, resist, sigma


def solution(mesh):
    in_specs = (P("cube", None), P(None, "cube", "col"), P(None, "col"), P(), P(), P())
    out_specs = (P(None, "cube", "col"), P(None, "cube", "col"), P("cube", None, "col"))
    return jax.shard_map(body, mesh=mesh, in_specs=in_specs, out_specs=out_specs, check_vma=False)
```

```python
import functools

import jax
import jax.numpy as jnp
from jax import lax
from jax.experimental import pallas as pl
from jax.experimental.pallas import tpu as pltpu
from jax.sharding import PartitionSpec as P

AXES = ("cube", "col")
F32 = jnp.float32
VMEM = pltpu.VMEM
SMEM = pltpu.SMEM
VLIM = 24
INFO = 144
COST = 4


def index_of(x, y, zl, zh, core):
    return ((y * 2 + zl) * 4 + x) * 8 + zh * 2 + core


def table(move):
    pairs = []
    for y in range(4):
        for zl in range(2):
            for x in range(4):
                for zh in range(4):
                    for core in range(2):
                        pairs.append(
                            (index_of(x, y, zl, zh, core), index_of(*move(x, y, zl, zh, core)))
                        )
    return pairs


def send_pq(v, dp, dq):
    def move(x, y, zl, zh, core):
        dx, dy = (dp, dq) if core == 0 else (dq, dp)
        return (x + dx) % 4, (y + dy) % 4, zl, zh, core

    return lax.ppermute(v, AXES, table(move))


def send_x(v, d):
    return lax.ppermute(v, AXES, table(lambda x, y, zl, zh, core: ((x + d) % 4, y, zl, zh, core)))


def send_x_flip(v, bit):
    return lax.ppermute(v, AXES, table(lambda x, y, zl, zh, core: (x ^ bit, y, zl, zh, core)))


def send_y(v, d):
    return lax.ppermute(v, AXES, table(lambda x, y, zl, zh, core: (x, (y + d) % 4, zl, zh, core)))


def send_pair(v):
    return lax.ppermute(v, AXES, table(lambda x, y, zl, zh, core: (x, y, 1 - zl, zh, core)))


def send_core(v):
    return lax.ppermute(v, AXES, table(lambda x, y, zl, zh, core: (x, y, zl, zh, 1 - core)))


def send_zh(v, d):
    return lax.ppermute(v, AXES, table(lambda x, y, zl, zh, core: (x, y, zl, (zh + d) % 4, core)))


def split(a):
    hi = a.astype(jnp.bfloat16)
    lo = (a - hi.astype(F32)).astype(jnp.bfloat16)
    return hi, lo


def dot3(a, b, dims):
    ah, al = split(a)
    bh, bl = split(b)
    dg = functools.partial(lax.dot_general, dimension_numbers=(dims, ((), ())),
                           preferred_element_type=F32)
    return dg(ah, bh) + (dg(ah, bl) + dg(al, bh))


def plan_kernel(tile_map, counts, assign, plan):
    me, col = lax.axis_index("cube"), lax.axis_index("col")
    x, zl, y = lax.rem(me, 4), lax.rem(lax.div(me, 4), 2), lax.div(me, 8)
    zh, core = lax.div(col, 2), lax.rem(col, 2)
    group = (y * 2 + zl) * 4
    flip = jnp.where(assign[0] != 0, 1, 0)
    for i, value in enumerate((x, y, zl, zh, core)):
        plan[INFO + i] = value

    def fill(i, _):
        s, dp, dq, plane = i & 1, (i >> 1) & 3, (i >> 3) & 3, i >> 5
        dx = jnp.where(core == 0, dp, dq)
        dy = jnp.where(core == 0, dq, dp)
        src = (((y - dy) & 3) * 2 + ((zl + plane) & 1)) * 4 + ((x - dx) & 3)
        front = s ^ flip
        tile = tile_map[front, src >> 1]
        plan[i] = tile * 2 + (src & 1)
        live = jnp.clip(counts[front] - src * 128, 0, 128)
        plan[64 + i] = live

        @pl.when((tile >= group) & (tile < group + 4))
        def _():
            piece = (tile - group) * 2 + (src & 1)
            plan[128 + piece] = i
            plan[136 + piece] = live

        return 0

    lax.fori_loop(0, 64, fill, 0, unroll=8)

    def look(i, _):
        front, j = i >> 4, i & 15
        tile = tile_map[front, j]

        @pl.when((tile >= group) & (tile < group + 4))
        def _():
            plan[INFO + 5 + ((x ^ tile) & 3)] = front ^ flip

        @pl.when(tile == me)
        def _():
            plan[INFO + 9] = front
            plan[INFO + 10] = jnp.clip(counts[front] - j * 256, 0, 256)

        return 0

    lax.fori_loop(0, 32, look, 0, unroll=8)
    plan[INFO + 11] = flip
    plan[INFO + 12] = me


def plan_call(tile_map, counts, assign):
    spec = pl.BlockSpec(memory_space=SMEM)
    return pl.pallas_call(
        plan_kernel,
        in_specs=[spec] * 3,
        out_specs=spec,
        out_shape=jax.ShapeDtypeStruct((160,), jnp.int32),
        compiler_params=pltpu.CompilerParams(vmem_limit_bytes=2**20),
        name="plan",
    )(tile_map, counts, assign)


def u_kernel(first, groups, plan, *refs):
    us, refs = refs[:len(groups)], refs[len(groups):]
    if not first:
        (own_in, ut_in), refs = refs[:2], refs[2:]
    own, ut, buf, turned, sem = refs

    def each(do):
        for piece in range(8):
            place = plan[128 + piece]
            for u, (base, size) in zip(us, groups):
                @pl.when((place >= base * 2) & (place < (base + size) * 2))
                def _():
                    at = place - base * 2
                    do(piece, pltpu.make_async_copy(u.at[at >> 1, at & 1], buf.at[piece],
                                                    sem.at[piece]))

    each(lambda piece, copy: copy.start())
    if first:
        own[...] = jnp.zeros_like(own)
        ut[...] = jnp.zeros_like(ut)
    else:
        own[...] = own_in[...]
        ut[...] = ut_in[...]
    x = plan[INFO]
    rows = lax.broadcasted_iota(jnp.int32, (128, 256), 0)

    def take(piece, copy):
        copy.wait()
        part = jnp.where(rows < plan[136 + piece], buf[piece], 0.0)
        turned[...] = part.T
        ut[piece] = turned[pl.ds(pl.multiple_of(x * 64, 64), 64), :]

        @pl.when(x == piece // 2)
        def _():
            half = piece % 2
            own[half * 128:(half + 1) * 128, :] = part

    each(take)


def u_call(plan, us, starts, carry):
    groups = tuple((start, u.shape[0]) for start, u in zip(starts, us))
    first = carry is None
    smem, vmem, anywhere = (pl.BlockSpec(memory_space=m) for m in (SMEM, VMEM, pl.ANY))
    at = 1 + len(us)
    return pl.pallas_call(
        functools.partial(u_kernel, first, groups),
        in_specs=[smem] + [anywhere] * len(us) + ([] if first else [vmem] * 2),
        out_specs=[vmem] * 2,
        out_shape=[jax.ShapeDtypeStruct((256, 256), F32), jax.ShapeDtypeStruct((8, 64, 128), F32)],
        scratch_shapes=[VMEM((8, 128, 256), F32), VMEM((256, 128), F32),
                        pltpu.SemaphoreType.DMA((8,))],
        input_output_aliases={} if first else {at: 0, at + 1: 1},
        compiler_params=pltpu.CompilerParams(vmem_limit_bytes=16 * 2**20),
        name="u_rows",
    )(plan, *us, *(() if first else carry))


def v_kernel(first, last, groups, plan, *refs):
    ginv, refs = refs[0], refs[1:]
    us, refs = refs[:len(groups)], refs[len(groups):]
    if not first:
        v_in, refs = refs[0], refs[1:]
    if last:
        own, refs = refs[0], refs[1:]
    v_out = refs[0]
    gbuf, ubuf, gsem, usem = refs[-4:]
    copies = []
    at = 0
    for i, (base, size) in enumerate(groups):
        mine = [pltpu.make_async_copy(us[i], ubuf.at[pl.ds(at, size)], usem.at[i])]
        for b in range(size):
            for s in range(2):
                column = pl.multiple_of(plan[(base + b) * 2 + s] * 128, 128)
                mine.append(pltpu.make_async_copy(
                    ginv.at[:, pl.ds(column, 128)],
                    gbuf.at[s, :, pl.ds((at + b) * 128, 128)],
                    gsem.at[(at + b) * 2 + s]))
        for c in mine:
            c.start()
        copies.append(mine)
        at += size
    rows = lax.broadcasted_iota(jnp.int32, (128, 256), 0)
    at = 0
    for i, (base, size) in enumerate(groups):
        for c in copies[i]:
            c.wait()
        for s in range(2):
            uu = jnp.concatenate(
                [jnp.where(rows < plan[64 + (base + b) * 2 + s], ubuf[at + b, s], 0.0)
                 for b in range(size)], axis=0)
            gg = gbuf[s, :, at * 128:(at + size) * 128]
            part = dot3(gg, uu, ((1,), (0,)))
            if i > 0:
                part += v_out[s]
            elif not first:
                part += v_in[s]
            v_out[s] = part
        at += size
    if last:
        msg = refs[1]
        v_own = v_out[plan[INFO + 9] ^ plan[INFO + 11]]
        msg[:256, :] = v_own
        diag = jnp.sum(own[...] * v_own, axis=0, keepdims=True)
        msg[256:264, :] = jnp.broadcast_to(diag, (8, 256))


def v_call(ginv, plan, us, starts, carry, own=None):
    groups = tuple((start, u.shape[0]) for start, u in zip(starts, us))
    n = sum(size for _, size in groups)
    first, last = carry is None, own is not None
    shapes = [(2, 256, 256)]
    smem, vmem, anywhere = (pl.BlockSpec(memory_space=m) for m in (SMEM, VMEM, pl.ANY))
    extra = [t for t in (carry, own) if t is not None]
    if last:
        shapes.append((264, 256))
    out = pl.pallas_call(
        functools.partial(v_kernel, first, last, groups),
        in_specs=[smem] + [pl.BlockSpec(memory_space=pltpu.HBM)] + [anywhere] * len(us)
        + [vmem] * len(extra),
        out_specs=[vmem] * len(shapes),
        out_shape=[jax.ShapeDtypeStruct(shape, F32) for shape in shapes],
        scratch_shapes=[VMEM((2, 256, n * 128), F32), VMEM((n, 2, 128, 256), F32),
                        pltpu.SemaphoreType.DMA((2 * n,)), pltpu.SemaphoreType.DMA((len(us),))],
        compiler_params=pltpu.CompilerParams(vmem_limit_bytes=VLIM * 2**20),
        cost_estimate=pl.CostEstimate(flops=3 * 4 * 256 * 128 * n * 256,
                                      bytes_accessed=n * COST * 2**20, transcendentals=0),
        name="v_part",
    )(plan, ginv, *us, *extra)
    return out if last else out[0]


def prod_kernel(plan, v01, v23, near, near2, far, far2, m0, m1, m2, m3, acc):
    x, y, zl, zh, core = plan[INFO], plan[INFO + 1], plan[INFO + 2], plan[INFO + 3], plan[INFO + 4]
    acc[...] = jnp.zeros_like(acc)
    vs = (v01.at[0], v01.at[1], v23.at[0], v23.at[1])
    order = [(k, side) for k in range(4) for side in range(2)]
    for t in range(4):
        tile = x ^ t
        left = []
        for k, side in order:
            u = (near2, far2)[side] if k == 2 else (near, far)[side].at[(0, 1, None, 2)[k]]
            left.append(jnp.concatenate([u[tile * 2 + h] for h in range(2)], axis=1))
        part = dot3(jnp.concatenate(left, axis=0), vs[t][:256, :], ((1,), (0,)))
        s = plan[INFO + 5 + t]
        for i, (k, side) in enumerate(order):
            block = lax.rem(zh + 4 - k, 4) * 2 + (core if side == 0 else 1 - core)
            acc[s, block] += part[i * 64:(i + 1) * 64, :]
    diag = []
    for s in range(2):
        total = None
        for t in range(4):
            term = jnp.where(plan[INFO + 5 + t] == s, vs[t][256:264, :], 0.0)
            total = term if total is None else total + term
        diag.append(total)
    for k, m in enumerate((m0, m1, m2, m3)):
        for zrel in range(2):
            for s in range(2):
                block = 2 * lax.rem(y + k, 4) + lax.rem(zl + zrel, 2)
                at = (zrel * 2 + s) * 64
                m[at:at + 64, :] = acc[s, block]
        m[256:264, :] = diag[0]
        m[264:272, :] = diag[1]


def prod_call(plan, vs, pieces):
    spec = pl.BlockSpec(memory_space=VMEM)
    return pl.pallas_call(
        prod_kernel,
        in_specs=[pl.BlockSpec(memory_space=SMEM)] + [spec] * 6,
        out_specs=[spec] * 4,
        out_shape=[jax.ShapeDtypeStruct((272, 256), F32)] * 4,
        scratch_shapes=[VMEM((2, 8, 64, 256), F32)],
        compiler_params=pltpu.CompilerParams(vmem_limit_bytes=24 * 2**20),
        cost_estimate=pl.CostEstimate(flops=3 * 2 * 512 * 1024 * 256, bytes_accessed=5 * 2**20,
                                      transcendentals=0),
        name="product",
    )(plan, *vs, *pieces)


def sum2_kernel(r0, r1, r2, r3, keep, away):
    for rows, o, to in ((0, keep, 0), (128, away, 0)):
        o[to:to + 128, :] = (r0[rows:rows + 128, :] + r1[rows:rows + 128, :]) + (
            r2[rows:rows + 128, :] + r3[rows:rows + 128, :])
    d = (r0[256:272, :] + r1[256:272, :]) + (r2[256:272, :] + r3[256:272, :])
    keep[128:144, :] = d
    away[128:144, :] = d


def sum2_call(rs):
    spec = pl.BlockSpec(memory_space=VMEM)
    return pl.pallas_call(
        sum2_kernel,
        in_specs=[spec] * 4,
        out_specs=[spec] * 2,
        out_shape=[jax.ShapeDtypeStruct((144, 256), F32)] * 2,
        compiler_params=pltpu.CompilerParams(vmem_limit_bytes=16 * 2**20),
        name="sum_second",
    )(*rs)


def cross_kernel(plan, v, block, cross, base):
    flip = plan[INFO + 11]
    eye = lax.broadcasted_iota(jnp.int32, (256, 256), 0) == lax.broadcasted_iota(
        jnp.int32, (256, 256), 1)
    g_diag = jnp.sum(jnp.where(eye, block[...], 0.0), axis=1, keepdims=True)
    for f in range(2):
        vf = v[f ^ flip]
        cross[f] = -vf
        base[f] = g_diag + 2.0 * vf


def cross_call(plan, v, ginv):
    full = pl.BlockSpec((2, 256, 256), lambda _, plan: (0, 0, 0))
    return pl.pallas_call(
        cross_kernel,
        grid_spec=pltpu.PrefetchScalarGridSpec(
            num_scalar_prefetch=1, grid=(1,),
            in_specs=[full, pl.BlockSpec((256, 256), lambda _, plan: (0, plan[INFO + 12]))],
            out_specs=[full, full],
        ),
        out_shape=[jax.ShapeDtypeStruct((2, 256, 256), F32)] * 2,
        compiler_params=pltpu.CompilerParams(vmem_limit_bytes=12 * 2**20),
        name="cross",
    )(plan, v, ginv)


def last_kernel(plan, keep, came, dinv, base, resist, sigma):
    flip = plan[INFO + 11]
    rows = lax.broadcasted_iota(jnp.int32, (256, 256), 0)
    at = lax.broadcasted_iota(jnp.int32, (64, 256), 0) + lax.rem(plan[INFO + 12], 4) * 64
    on_diag = at == lax.broadcasted_iota(jnp.int32, (64, 256), 1)
    on_diag = on_diag & (plan[INFO + 12] // 4 == plan[INFO + 3] * 2 + plan[INFO + 4])
    for f in range(2):
        s = f ^ flip
        d = dinv[pl.ds(s, 1), :]
        total = keep[pl.ds(pl.multiple_of(s * 64, 64), 64), :] + came[
            pl.ds(pl.multiple_of(s * 64, 64), 64), :]
        sigma[:, f, :] = total + jnp.where(on_diag, d, 0.0)
        deep = pl.ds(pl.multiple_of(128 + s * 8, 8), 8)
        diag = (keep[deep, :] + came[deep, :])[0:1, :] + d
        live = jnp.where(plan[INFO + 9] == f, plan[INFO + 10], 0)
        resist[f] = jnp.where(rows < live, diag + base[f], 0.0)


def last_call(plan, keep, came, dinv, base):
    spec = pl.BlockSpec(memory_space=VMEM)
    return pl.pallas_call(
        last_kernel,
        in_specs=[pl.BlockSpec(memory_space=SMEM)] + [spec] * 4,
        out_specs=[spec] * 2,
        out_shape=[jax.ShapeDtypeStruct((2, 256, 256), F32), jax.ShapeDtypeStruct((64, 2, 256), F32)],
        compiler_params=pltpu.CompilerParams(vmem_limit_bytes=12 * 2**20),
        name="last",
    )(plan, keep, came, dinv, base)


def body(ginv, ufactor, dinv, tile_map, counts, assign):
    pin = lax.optimization_barrier

    a0 = ufactor
    b0 = send_pair(a0)
    plan = plan_call(tile_map, counts, assign)
    a1, a2, a3 = send_pq(a0, 1, 0), send_pq(a0, 2, 0), send_pq(a0, -1, 0)
    b1, b2, b3 = send_pq(b0, 1, 0), send_pq(b0, 2, 0), send_pq(b0, -1, 0)
    a1, a2, a3, b0, b1, b2, b3 = pin((a1, a2, a3, b0, b1, b2, b3))
    ga = jnp.stack([a0, a1, a2, a3])
    ga1 = send_pq(ga, 0, 1)
    ga3 = send_pq(ga, 0, -1)
    gb = jnp.stack([b0, b1, b2, b3])
    gb1 = send_pq(gb[:3], 0, 1)
    gb3 = send_pq(gb[1:], 0, -1)
    carry = v_call(ginv, plan, [ga], [0], None)
    ga1, ga3, carry = pin((ga1, ga3, carry))
    ga2a = send_pq(ga1[:2], 0, 1)
    ga2b = send_pq(ga3[2:], 0, -1)
    gbr = send_pair(jnp.concatenate([ga1[3:], ga3[:1]]))
    carry = v_call(ginv, plan, [gb, ga1, ga3], [16, 4, 12], carry)
    gb1, gb3, carry = pin((gb1, gb3, carry))
    gb2a = send_pq(gb1[:2], 0, 1)
    gb2b = send_pq(gb3[1:], 0, -1)
    carry = v_call(ginv, plan, [gb1, gb3], [20, 29], carry)
    ga2a, ga2b, gbr, carry = pin((ga2a, ga2b, gbr, carry))
    gbr1, gbr3 = gbr[:1], gbr[1:]
    rows = u_call(plan, [ga, gb, ga1, ga3, gb1, gbr1, gbr3, gb3, ga2a, ga2b],
                  [0, 16, 4, 12, 20, 23, 28, 29, 8, 10], None)
    gb2a, gb2b, carry, rows = pin((gb2a, gb2b, carry, rows))
    own, ut = u_call(plan, [gb2a, gb2b], [24, 26], rows)

    c1, c3 = send_zh(ut, 1), send_zh(ut, -1)
    v, msg = v_call(ginv, plan, [ga2a, ga2b, gbr1, gbr3, gb2a, gb2b], [8, 10, 23, 28, 24, 26],
                    carry, own)
    v01 = jnp.stack([msg, send_x_flip(msg, 1)])
    v23 = send_x_flip(v01, 2)
    c1, c3, ut, _ = pin((c1, c3, ut, msg))
    c2 = jnp.concatenate([send_zh(c1[:4], 1), send_zh(c3[4:], -1)])
    near = [jnp.stack([ut, c1, c3]), c2]
    far = [send_core(t) for t in near]
    cross, base = cross_call(plan, v, ginv)

    m = prod_call(plan, [v01, v23], near + far)
    m2 = send_y(m[2], 2)
    r = [m[0], send_y(m[1], 1), m2, send_y(m[3], -1)]
    keep, away = sum2_call(r)
    came = send_pair(away)
    resist, sigma = last_call(plan, keep, came, dinv, base)
    return cross, resist, sigma


def solution(mesh):
    in_specs = (P("cube", None), P(None, "cube", "col"), P(None, "col"), P(), P(), P())
    out_specs = (P(None, "cube", "col"), P(None, "cube", "col"), P("cube", None, "col"))
    return jax.shard_map(body, mesh=mesh, in_specs=in_specs, out_specs=out_specs, check_vma=False)
```

```python
import functools

import jax
import jax.numpy as jnp
from jax import lax
from jax.experimental import pallas as pl
from jax.experimental.pallas import tpu as pltpu
from jax.sharding import PartitionSpec as P

AXES = ("cube", "col")
F32 = jnp.float32
VMEM = pltpu.VMEM
SMEM = pltpu.SMEM
VLIM = 24
INFO = 144
COST = 4


def index_of(x, y, zl, zh, core):
    return ((y * 2 + zl) * 4 + x) * 8 + zh * 2 + core


def table(move):
    pairs = []
    for y in range(4):
        for zl in range(2):
            for x in range(4):
                for zh in range(4):
                    for core in range(2):
                        pairs.append(
                            (index_of(x, y, zl, zh, core), index_of(*move(x, y, zl, zh, core)))
                        )
    return pairs


def send_pq(v, dp, dq):
    def move(x, y, zl, zh, core):
        dx, dy = (dp, dq) if core == 0 else (dq, dp)
        return (x + dx) % 4, (y + dy) % 4, zl, zh, core

    return lax.ppermute(v, AXES, table(move))


def send_x(v, d):
    return lax.ppermute(v, AXES, table(lambda x, y, zl, zh, core: ((x + d) % 4, y, zl, zh, core)))


def send_x_flip(v, bit):
    return lax.ppermute(v, AXES, table(lambda x, y, zl, zh, core: (x ^ bit, y, zl, zh, core)))


def send_y(v, d):
    return lax.ppermute(v, AXES, table(lambda x, y, zl, zh, core: (x, (y + d) % 4, zl, zh, core)))


def send_yz(v, dy, dz):
    return lax.ppermute(v, AXES, table(lambda x, y, zl, zh, core: (x, (y + dy) % 4, zl ^ dz, zh, core)))


def send_pair(v):
    return lax.ppermute(v, AXES, table(lambda x, y, zl, zh, core: (x, y, 1 - zl, zh, core)))


def send_core(v):
    return lax.ppermute(v, AXES, table(lambda x, y, zl, zh, core: (x, y, zl, zh, 1 - core)))


def send_zh(v, d):
    return lax.ppermute(v, AXES, table(lambda x, y, zl, zh, core: (x, y, zl, (zh + d) % 4, core)))


def split(a):
    hi = a.astype(jnp.bfloat16)
    lo = (a - hi.astype(F32)).astype(jnp.bfloat16)
    return hi, lo


def dot3(a, b, dims):
    ah, al = split(a)
    bh, bl = split(b)
    dg = functools.partial(lax.dot_general, dimension_numbers=(dims, ((), ())),
                           preferred_element_type=F32)
    return dg(ah, bh) + (dg(ah, bl) + dg(al, bh))


def plan_kernel(tile_map, counts, assign, plan):
    me, col = lax.axis_index("cube"), lax.axis_index("col")
    x, zl, y = lax.rem(me, 4), lax.rem(lax.div(me, 4), 2), lax.div(me, 8)
    zh, core = lax.div(col, 2), lax.rem(col, 2)
    group = (y * 2 + zl) * 4
    flip = jnp.where(assign[0] != 0, 1, 0)
    for i, value in enumerate((x, y, zl, zh, core)):
        plan[INFO + i] = value

    def fill(i, _):
        s, dp, dq, plane = i & 1, (i >> 1) & 3, (i >> 3) & 3, i >> 5
        dx = jnp.where(core == 0, dp, dq)
        dy = jnp.where(core == 0, dq, dp)
        src = (((y - dy) & 3) * 2 + ((zl + plane) & 1)) * 4 + ((x - dx) & 3)
        front = s ^ flip
        tile = tile_map[front, src >> 1]
        plan[i] = tile * 2 + (src & 1)
        live = jnp.clip(counts[front] - src * 128, 0, 128)
        plan[64 + i] = live

        @pl.when((tile >= group) & (tile < group + 4))
        def _():
            piece = (tile - group) * 2 + (src & 1)
            plan[128 + piece] = i
            plan[136 + piece] = live

        return 0

    lax.fori_loop(0, 64, fill, 0, unroll=8)

    def look(i, _):
        front, j = i >> 4, i & 15
        tile = tile_map[front, j]

        @pl.when((tile >= group) & (tile < group + 4))
        def _():
            plan[INFO + 5 + ((x ^ tile) & 3)] = front ^ flip

        @pl.when(tile == me)
        def _():
            plan[INFO + 9] = front
            plan[INFO + 10] = jnp.clip(counts[front] - j * 256, 0, 256)

        return 0

    lax.fori_loop(0, 32, look, 0, unroll=8)
    plan[INFO + 11] = flip
    plan[INFO + 12] = me


def plan_call(tile_map, counts, assign):
    spec = pl.BlockSpec(memory_space=SMEM)
    return pl.pallas_call(
        plan_kernel,
        in_specs=[spec] * 3,
        out_specs=spec,
        out_shape=jax.ShapeDtypeStruct((160,), jnp.int32),
        compiler_params=pltpu.CompilerParams(vmem_limit_bytes=2**20),
        name="plan",
    )(tile_map, counts, assign)


def u_kernel(first, groups, plan, *refs):
    us, refs = refs[:len(groups)], refs[len(groups):]
    if not first:
        (own_in, ut_in), refs = refs[:2], refs[2:]
    own, ut, buf, turned, sem = refs

    def each(do):
        for piece in range(8):
            place = plan[128 + piece]
            for u, (base, size) in zip(us, groups):
                @pl.when((place >= base * 2) & (place < (base + size) * 2))
                def _():
                    at = place - base * 2
                    do(piece, pltpu.make_async_copy(u.at[at >> 1, at & 1], buf.at[piece],
                                                    sem.at[piece]))

    each(lambda piece, copy: copy.start())
    if first:
        own[...] = jnp.zeros_like(own)
        ut[...] = jnp.zeros_like(ut)
    else:
        own[...] = own_in[...]
        ut[...] = ut_in[...]
    x = plan[INFO]
    rows = lax.broadcasted_iota(jnp.int32, (128, 256), 0)

    def take(piece, copy):
        copy.wait()
        part = jnp.where(rows < plan[136 + piece], buf[piece], 0.0)
        turned[...] = part.T
        ut[piece] = turned[pl.ds(pl.multiple_of(x * 64, 64), 64), :]

        @pl.when(x == piece // 2)
        def _():
            half = piece % 2
            own[half * 128:(half + 1) * 128, :] = part

    each(take)


def u_call(plan, us, starts, carry):
    groups = tuple((start, u.shape[0]) for start, u in zip(starts, us))
    first = carry is None
    smem, vmem, anywhere = (pl.BlockSpec(memory_space=m) for m in (SMEM, VMEM, pl.ANY))
    at = 1 + len(us)
    return pl.pallas_call(
        functools.partial(u_kernel, first, groups),
        in_specs=[smem] + [anywhere] * len(us) + ([] if first else [vmem] * 2),
        out_specs=[vmem] * 2,
        out_shape=[jax.ShapeDtypeStruct((256, 256), F32), jax.ShapeDtypeStruct((8, 64, 128), F32)],
        scratch_shapes=[VMEM((8, 128, 256), F32), VMEM((256, 128), F32),
                        pltpu.SemaphoreType.DMA((8,))],
        input_output_aliases={} if first else {at: 0, at + 1: 1},
        compiler_params=pltpu.CompilerParams(vmem_limit_bytes=16 * 2**20),
        name="u_rows",
    )(plan, *us, *(() if first else carry))


def v_kernel(first, last, groups, plan, *refs):
    ginv, refs = refs[0], refs[1:]
    us, refs = refs[:len(groups)], refs[len(groups):]
    if not first:
        v_in, refs = refs[0], refs[1:]
    if last:
        own, refs = refs[0], refs[1:]
    v_out = refs[0]
    gbuf, ubuf, gsem, usem = refs[-4:]
    copies = []
    at = 0
    for i, (base, size) in enumerate(groups):
        mine = [pltpu.make_async_copy(us[i], ubuf.at[pl.ds(at, size)], usem.at[i])]
        for b in range(size):
            for s in range(2):
                column = pl.multiple_of(plan[(base + b) * 2 + s] * 128, 128)
                mine.append(pltpu.make_async_copy(
                    ginv.at[:, pl.ds(column, 128)],
                    gbuf.at[s, :, pl.ds((at + b) * 128, 128)],
                    gsem.at[(at + b) * 2 + s]))
        for c in mine:
            c.start()
        copies.append(mine)
        at += size
    rows = lax.broadcasted_iota(jnp.int32, (128, 256), 0)
    at = 0
    for i, (base, size) in enumerate(groups):
        for c in copies[i]:
            c.wait()
        for s in range(2):
            uu = jnp.concatenate(
                [jnp.where(rows < plan[64 + (base + b) * 2 + s], ubuf[at + b, s], 0.0)
                 for b in range(size)], axis=0)
            gg = gbuf[s, :, at * 128:(at + size) * 128]
            part = dot3(gg, uu, ((1,), (0,)))
            if i > 0:
                part += v_out[s]
            elif not first:
                part += v_in[s]
            v_out[s] = part
        at += size
    if last:
        msg = refs[1]
        v_own = v_out[plan[INFO + 9] ^ plan[INFO + 11]]
        msg[:256, :] = v_own
        diag = jnp.sum(own[...] * v_own, axis=0, keepdims=True)
        msg[256:264, :] = jnp.broadcast_to(diag, (8, 256))


def v_call(ginv, plan, us, starts, carry, own=None):
    groups = tuple((start, u.shape[0]) for start, u in zip(starts, us))
    n = sum(size for _, size in groups)
    first, last = carry is None, own is not None
    shapes = [(2, 256, 256)]
    smem, vmem, anywhere = (pl.BlockSpec(memory_space=m) for m in (SMEM, VMEM, pl.ANY))
    extra = [t for t in (carry, own) if t is not None]
    if last:
        shapes.append((264, 256))
    out = pl.pallas_call(
        functools.partial(v_kernel, first, last, groups),
        in_specs=[smem] + [pl.BlockSpec(memory_space=pltpu.HBM)] + [anywhere] * len(us)
        + [vmem] * len(extra),
        out_specs=[vmem] * len(shapes),
        out_shape=[jax.ShapeDtypeStruct(shape, F32) for shape in shapes],
        scratch_shapes=[VMEM((2, 256, n * 128), F32), VMEM((n, 2, 128, 256), F32),
                        pltpu.SemaphoreType.DMA((2 * n,)), pltpu.SemaphoreType.DMA((len(us),))],
        compiler_params=pltpu.CompilerParams(vmem_limit_bytes=VLIM * 2**20),
        cost_estimate=pl.CostEstimate(flops=3 * 4 * 256 * 128 * n * 256,
                                      bytes_accessed=n * COST * 2**20, transcendentals=0),
        name="v_part",
    )(plan, ginv, *us, *extra)
    return out if last else out[0]


def prod_kernel(plan, v01, v23, near, near2, far, far2, *refs):
    *ms, acc = refs
    x, y, zl, zh, core = plan[INFO], plan[INFO + 1], plan[INFO + 2], plan[INFO + 3], plan[INFO + 4]
    acc[...] = jnp.zeros_like(acc)
    vs = (v01.at[0], v01.at[1], v23.at[0], v23.at[1])
    order = [(k, side) for k in range(4) for side in range(2)]
    for t in range(4):
        tile = x ^ t
        left = []
        for k, side in order:
            u = (near2, far2)[side] if k == 2 else (near, far)[side].at[(0, 1, None, 2)[k]]
            left.append(jnp.concatenate([u[tile * 2 + h] for h in range(2)], axis=1))
        part = dot3(jnp.concatenate(left, axis=0), vs[t][:256, :], ((1,), (0,)))
        s = plan[INFO + 5 + t]
        for i, (k, side) in enumerate(order):
            block = lax.rem(zh + 4 - k, 4) * 2 + (core if side == 0 else 1 - core)
            acc[s, block] += part[i * 64:(i + 1) * 64, :]
    diag = []
    for s in range(2):
        total = None
        for t in range(4):
            term = jnp.where(plan[INFO + 5 + t] == s, vs[t][256:264, :], 0.0)
            total = term if total is None else total + term
        diag.append(total)
    for k in range(4):
        for zrel in range(2):
            m = ms[k * 2 + zrel]
            for s in range(2):
                m[s * 64:(s + 1) * 64, :] = acc[s, 2 * lax.rem(y + k, 4) + (zl ^ zrel)]
                m[128 + s * 8:136 + s * 8, :] = diag[s]


def prod_call(plan, vs, pieces):
    spec = pl.BlockSpec(memory_space=VMEM)
    return pl.pallas_call(
        prod_kernel,
        in_specs=[pl.BlockSpec(memory_space=SMEM)] + [spec] * 6,
        out_specs=[spec] * 8,
        out_shape=[jax.ShapeDtypeStruct((144, 256), F32)] * 8,
        scratch_shapes=[VMEM((2, 8, 64, 256), F32)],
        compiler_params=pltpu.CompilerParams(vmem_limit_bytes=24 * 2**20),
        cost_estimate=pl.CostEstimate(flops=3 * 2 * 512 * 1024 * 256, bytes_accessed=5 * 2**20,
                                      transcendentals=0),
        name="product",
    )(plan, *vs, *pieces)


def cross_kernel(plan, v, block, cross, base):
    flip = plan[INFO + 11]
    eye = lax.broadcasted_iota(jnp.int32, (256, 256), 0) == lax.broadcasted_iota(
        jnp.int32, (256, 256), 1)
    g_diag = jnp.sum(jnp.where(eye, block[...], 0.0), axis=1, keepdims=True)
    for f in range(2):
        vf = v[f ^ flip]
        cross[f] = -vf
        base[f] = g_diag + 2.0 * vf


def cross_call(plan, v, ginv):
    full = pl.BlockSpec((2, 256, 256), lambda _, plan: (0, 0, 0))
    return pl.pallas_call(
        cross_kernel,
        grid_spec=pltpu.PrefetchScalarGridSpec(
            num_scalar_prefetch=1, grid=(1,),
            in_specs=[full, pl.BlockSpec((256, 256), lambda _, plan: (0, plan[INFO + 12]))],
            out_specs=[full, full],
        ),
        out_shape=[jax.ShapeDtypeStruct((2, 256, 256), F32)] * 2,
        compiler_params=pltpu.CompilerParams(vmem_limit_bytes=12 * 2**20),
        name="cross",
    )(plan, v, ginv)


def last_kernel(plan, dinv, base, *refs):
    *ms, resist, sigma, total = refs
    sums = [ms[i][...] + ms[i + 1][...] for i in range(0, 8, 2)]
    total[...] = (sums[0] + sums[1]) + (sums[2] + sums[3])
    flip = plan[INFO + 11]
    rows = lax.broadcasted_iota(jnp.int32, (256, 256), 0)
    at = lax.broadcasted_iota(jnp.int32, (64, 256), 0) + lax.rem(plan[INFO + 12], 4) * 64
    on_diag = at == lax.broadcasted_iota(jnp.int32, (64, 256), 1)
    on_diag = on_diag & (plan[INFO + 12] // 4 == plan[INFO + 3] * 2 + plan[INFO + 4])
    for f in range(2):
        s = f ^ flip
        d = dinv[pl.ds(s, 1), :]
        sigma[:, f, :] = total[pl.ds(pl.multiple_of(s * 64, 64), 64), :] + jnp.where(on_diag, d, 0.0)
        deep = pl.ds(pl.multiple_of(128 + s * 8, 8), 8)
        diag = total[deep, :][0:1, :] + d
        live = jnp.where(plan[INFO + 9] == f, plan[INFO + 10], 0)
        resist[f] = jnp.where(rows < live, diag + base[f], 0.0)


def last_call(plan, dinv, base, ms):
    spec = pl.BlockSpec(memory_space=VMEM)
    return pl.pallas_call(
        last_kernel,
        in_specs=[pl.BlockSpec(memory_space=SMEM)] + [spec] * 10,
        out_specs=[spec] * 2,
        scratch_shapes=[VMEM((144, 256), F32)],
        out_shape=[jax.ShapeDtypeStruct((2, 256, 256), F32), jax.ShapeDtypeStruct((64, 2, 256), F32)],
        compiler_params=pltpu.CompilerParams(vmem_limit_bytes=12 * 2**20),
        name="last",
    )(plan, dinv, base, *ms)


def body(ginv, ufactor, dinv, tile_map, counts, assign):
    pin = lax.optimization_barrier

    a0 = ufactor
    b0 = send_pair(a0)
    plan = plan_call(tile_map, counts, assign)
    a1, a2, a3 = send_pq(a0, 1, 0), send_pq(a0, 2, 0), send_pq(a0, -1, 0)
    b1, b3 = send_pq(b0, 1, 0), send_pq(b0, -1, 0)
    a1, a2, a3, b0, b1, b3 = pin((a1, a2, a3, b0, b1, b3))
    ga = jnp.stack([a0, a1, a2, a3])
    ga1 = send_pq(ga, 0, 1)
    ga3 = send_pq(ga, 0, -1)
    b2, plan = pin((send_pair(a2), plan))
    gb = jnp.stack([b0, b1, b2, b3])
    gb1 = send_pq(gb[:3], 0, 1)
    gb3 = send_pq(gb[1:], 0, -1)
    carry = v_call(ginv, plan, [ga], [0], None)
    ga1, ga3, carry = pin((ga1, ga3, carry))
    ga2a = send_pq(ga1[:2], 0, 1)
    ga2b = send_pq(ga3[2:], 0, -1)
    gbr = send_pair(jnp.concatenate([ga1[3:], ga3[:1]]))
    carry = v_call(ginv, plan, [gb, ga1, ga3], [16, 4, 12], carry)
    gb1, gb3, carry = pin((gb1, gb3, carry))
    gb2a = send_pq(gb1[:2], 0, 1)
    gb2b = send_pq(gb3[1:], 0, -1)
    carry = v_call(ginv, plan, [gb1, gb3], [20, 29], carry)
    ga2a, ga2b, gbr, carry = pin((ga2a, ga2b, gbr, carry))
    gbr1, gbr3 = gbr[:1], gbr[1:]
    rows = u_call(plan, [ga, gb, ga1, ga3, gb1, gbr1, gbr3, gb3, ga2a, ga2b],
                  [0, 16, 4, 12, 20, 23, 28, 29, 8, 10], None)
    gb2a, gb2b, carry, rows = pin((gb2a, gb2b, carry, rows))
    own, ut = u_call(plan, [gb2a, gb2b], [24, 26], rows)

    c1, c3 = send_zh(ut, 1), send_zh(ut, -1)
    v, msg = v_call(ginv, plan, [ga2a, ga2b, gbr1, gbr3, gb2a, gb2b], [8, 10, 23, 28, 24, 26],
                    carry, own)
    v01 = jnp.stack([msg, send_x_flip(msg, 1)])
    v23 = send_x_flip(v01, 2)
    c1, c3, ut, _ = pin((c1, c3, ut, msg))
    c2 = jnp.concatenate([send_zh(c1[:4], 1), send_zh(c3[4:], -1)])
    near = [jnp.stack([ut, c1, c3]), c2]
    far = [send_core(t) for t in near]
    cross, base = cross_call(plan, v, ginv)

    m = prod_call(plan, [v01, v23], near + far)
    r = [m[0]] + [send_yz(m[k * 2 + dz], k, dz) for k in (2, 1, 3, 0) for dz in (1, 0) if k or dz]
    resist, sigma = last_call(plan, dinv, base, r)
    return cross, resist, sigma


def solution(mesh):
    in_specs = (P("cube", None), P(None, "cube", "col"), P(None, "col"), P(), P(), P())
    out_specs = (P(None, "cube", "col"), P(None, "cube", "col"), P("cube", None, "col"))
    return jax.shard_map(body, mesh=mesh, in_specs=in_specs, out_specs=out_specs, check_vma=False)
```

```python
import functools

import jax
import jax.numpy as jnp
from jax import lax
from jax.experimental import pallas as pl
from jax.experimental.pallas import tpu as pltpu
from jax.sharding import PartitionSpec as P

AXES = ("cube", "col")
F32 = jnp.float32
VMEM = pltpu.VMEM
SMEM = pltpu.SMEM
VLIM = 24
INFO = 144
COST = 4


def index_of(x, y, zl, zh, core):
    return ((y * 2 + zl) * 4 + x) * 8 + zh * 2 + core


def table(move):
    pairs = []
    for y in range(4):
        for zl in range(2):
            for x in range(4):
                for zh in range(4):
                    for core in range(2):
                        pairs.append(
                            (index_of(x, y, zl, zh, core), index_of(*move(x, y, zl, zh, core)))
                        )
    return pairs


def send_pq(v, dp, dq):
    def move(x, y, zl, zh, core):
        dx, dy = (dp, dq) if core == 0 else (dq, dp)
        return (x + dx) % 4, (y + dy) % 4, zl, zh, core

    return lax.ppermute(v, AXES, table(move))


def send_x(v, d):
    return lax.ppermute(v, AXES, table(lambda x, y, zl, zh, core: ((x + d) % 4, y, zl, zh, core)))


def send_x_flip(v, bit):
    return lax.ppermute(v, AXES, table(lambda x, y, zl, zh, core: (x ^ bit, y, zl, zh, core)))


def send_y(v, d):
    return lax.ppermute(v, AXES, table(lambda x, y, zl, zh, core: (x, (y + d) % 4, zl, zh, core)))


def send_yz(v, dy, dz):
    return lax.ppermute(v, AXES, table(lambda x, y, zl, zh, core: (x, (y + dy) % 4, zl ^ dz, zh, core)))


def send_pair(v):
    return lax.ppermute(v, AXES, table(lambda x, y, zl, zh, core: (x, y, 1 - zl, zh, core)))


def send_core(v):
    return lax.ppermute(v, AXES, table(lambda x, y, zl, zh, core: (x, y, zl, zh, 1 - core)))


def send_zh(v, d):
    return lax.ppermute(v, AXES, table(lambda x, y, zl, zh, core: (x, y, zl, (zh + d) % 4, core)))


def split(a):
    hi = a.astype(jnp.bfloat16)
    lo = (a - hi.astype(F32)).astype(jnp.bfloat16)
    return hi, lo


def dot3(a, b, dims):
    ah, al = split(a)
    bh, bl = split(b)
    dg = functools.partial(lax.dot_general, dimension_numbers=(dims, ((), ())),
                           preferred_element_type=F32)
    return dg(ah, bh) + (dg(ah, bl) + dg(al, bh))


def plan_kernel(tile_map, counts, assign, plan):
    me, col = lax.axis_index("cube"), lax.axis_index("col")
    x, zl, y = lax.rem(me, 4), lax.rem(lax.div(me, 4), 2), lax.div(me, 8)
    zh, core = lax.div(col, 2), lax.rem(col, 2)
    group = (y * 2 + zl) * 4
    flip = jnp.where(assign[0] != 0, 1, 0)
    for i, value in enumerate((x, y, zl, zh, core)):
        plan[INFO + i] = value

    def fill(i, _):
        s, dp, dq, plane = i & 1, (i >> 1) & 3, (i >> 3) & 3, i >> 5
        dx = jnp.where(core == 0, dp, dq)
        dy = jnp.where(core == 0, dq, dp)
        src = (((y - dy) & 3) * 2 + ((zl + plane) & 1)) * 4 + ((x - dx) & 3)
        front = s ^ flip
        tile = tile_map[front, src >> 1]
        plan[i] = tile * 2 + (src & 1)
        live = jnp.clip(counts[front] - src * 128, 0, 128)
        plan[64 + i] = live

        @pl.when((tile >= group) & (tile < group + 4))
        def _():
            piece = (tile - group) * 2 + (src & 1)
            plan[128 + piece] = i
            plan[136 + piece] = live

        return 0

    lax.fori_loop(0, 64, fill, 0, unroll=8)

    def look(i, _):
        front, j = i >> 4, i & 15
        tile = tile_map[front, j]

        @pl.when((tile >= group) & (tile < group + 4))
        def _():
            plan[INFO + 5 + ((x - tile) & 3)] = front ^ flip

        @pl.when(tile == me)
        def _():
            plan[INFO + 9] = front
            plan[INFO + 10] = jnp.clip(counts[front] - j * 256, 0, 256)

        return 0

    lax.fori_loop(0, 32, look, 0, unroll=8)
    plan[INFO + 11] = flip
    plan[INFO + 12] = me


def plan_call(tile_map, counts, assign):
    spec = pl.BlockSpec(memory_space=SMEM)
    return pl.pallas_call(
        plan_kernel,
        in_specs=[spec] * 3,
        out_specs=spec,
        out_shape=jax.ShapeDtypeStruct((160,), jnp.int32),
        compiler_params=pltpu.CompilerParams(vmem_limit_bytes=2**20),
        name="plan",
    )(tile_map, counts, assign)


def u_kernel(first, groups, plan, *refs):
    us, refs = refs[:len(groups)], refs[len(groups):]
    if not first:
        (own_in, ut_in), refs = refs[:2], refs[2:]
    own, ut, buf, turned, sem = refs

    def each(do):
        for piece in range(8):
            place = plan[128 + piece]
            for u, (base, size) in zip(us, groups):
                @pl.when((place >= base * 2) & (place < (base + size) * 2))
                def _():
                    at = place - base * 2
                    do(piece, pltpu.make_async_copy(u.at[at >> 1, at & 1], buf.at[piece],
                                                    sem.at[piece]))

    each(lambda piece, copy: copy.start())
    if first:
        own[...] = jnp.zeros_like(own)
        ut[...] = jnp.zeros_like(ut)
    else:
        own[...] = own_in[...]
        ut[...] = ut_in[...]
    x = plan[INFO]
    rows = lax.broadcasted_iota(jnp.int32, (128, 256), 0)

    def take(piece, copy):
        copy.wait()
        part = jnp.where(rows < plan[136 + piece], buf[piece], 0.0)
        turned[...] = part.T
        ut[piece] = turned[pl.ds(pl.multiple_of(x * 64, 64), 64), :]

        @pl.when(x == piece // 2)
        def _():
            half = piece % 2
            own[half * 128:(half + 1) * 128, :] = part

    each(take)


def u_call(plan, us, starts, carry):
    groups = tuple((start, u.shape[0]) for start, u in zip(starts, us))
    first = carry is None
    smem, vmem, anywhere = (pl.BlockSpec(memory_space=m) for m in (SMEM, VMEM, pl.ANY))
    at = 1 + len(us)
    return pl.pallas_call(
        functools.partial(u_kernel, first, groups),
        in_specs=[smem] + [anywhere] * len(us) + ([] if first else [vmem] * 2),
        out_specs=[vmem] * 2,
        out_shape=[jax.ShapeDtypeStruct((256, 256), F32), jax.ShapeDtypeStruct((8, 64, 128), F32)],
        scratch_shapes=[VMEM((8, 128, 256), F32), VMEM((256, 128), F32),
                        pltpu.SemaphoreType.DMA((8,))],
        input_output_aliases={} if first else {at: 0, at + 1: 1},
        compiler_params=pltpu.CompilerParams(vmem_limit_bytes=16 * 2**20),
        name="u_rows",
    )(plan, *us, *(() if first else carry))


def v_kernel(first, last, groups, plan, *refs):
    ginv, refs = refs[0], refs[1:]
    us, refs = refs[:len(groups)], refs[len(groups):]
    if not first:
        v_in, refs = refs[0], refs[1:]
    if last:
        own, refs = refs[0], refs[1:]
    v_out = refs[0]
    gbuf, ubuf, gsem, usem = refs[-4:]
    copies = []
    at = 0
    for i, (base, size) in enumerate(groups):
        mine = [pltpu.make_async_copy(us[i], ubuf.at[pl.ds(at, size)], usem.at[i])]
        for b in range(size):
            for s in range(2):
                column = pl.multiple_of(plan[(base + b) * 2 + s] * 128, 128)
                mine.append(pltpu.make_async_copy(
                    ginv.at[:, pl.ds(column, 128)],
                    gbuf.at[s, :, pl.ds((at + b) * 128, 128)],
                    gsem.at[(at + b) * 2 + s]))
        for c in mine:
            c.start()
        copies.append(mine)
        at += size
    rows = lax.broadcasted_iota(jnp.int32, (128, 256), 0)
    at = 0
    for i, (base, size) in enumerate(groups):
        for c in copies[i]:
            c.wait()
        for s in range(2):
            uu = jnp.concatenate(
                [jnp.where(rows < plan[64 + (base + b) * 2 + s], ubuf[at + b, s], 0.0)
                 for b in range(size)], axis=0)
            gg = gbuf[s, :, at * 128:(at + size) * 128]
            part = dot3(gg, uu, ((1,), (0,)))
            if i > 0:
                part += v_out[s]
            elif not first:
                part += v_in[s]
            v_out[s] = part
        at += size
    if last:
        msg = refs[1]
        v_own = v_out[plan[INFO + 9] ^ plan[INFO + 11]]
        msg[:256, :] = v_own
        diag = jnp.sum(own[...] * v_own, axis=0, keepdims=True)
        msg[256:264, :] = jnp.broadcast_to(diag, (8, 256))


def v_call(ginv, plan, us, starts, carry, own=None):
    groups = tuple((start, u.shape[0]) for start, u in zip(starts, us))
    n = sum(size for _, size in groups)
    first, last = carry is None, own is not None
    shapes = [(2, 256, 256)]
    smem, vmem, anywhere = (pl.BlockSpec(memory_space=m) for m in (SMEM, VMEM, pl.ANY))
    extra = [t for t in (carry, own) if t is not None]
    if last:
        shapes.append((264, 256))
    out = pl.pallas_call(
        functools.partial(v_kernel, first, last, groups),
        in_specs=[smem] + [pl.BlockSpec(memory_space=pltpu.HBM)] + [anywhere] * len(us)
        + [vmem] * len(extra),
        out_specs=[vmem] * len(shapes),
        out_shape=[jax.ShapeDtypeStruct(shape, F32) for shape in shapes],
        scratch_shapes=[VMEM((2, 256, n * 128), F32), VMEM((n, 2, 128, 256), F32),
                        pltpu.SemaphoreType.DMA((2 * n,)), pltpu.SemaphoreType.DMA((len(us),))],
        compiler_params=pltpu.CompilerParams(vmem_limit_bytes=VLIM * 2**20),
        cost_estimate=pl.CostEstimate(flops=3 * 4 * 256 * 128 * n * 256,
                                      bytes_accessed=n * COST * 2**20, transcendentals=0),
        name="v_part",
    )(plan, ginv, *us, *extra)
    return out if last else out[0]


def prod_kernel(plan, vs, near, near2, far, far2, *refs):
    *ms, acc = refs
    x, y, zl, zh, core = plan[INFO], plan[INFO + 1], plan[INFO + 2], plan[INFO + 3], plan[INFO + 4]
    acc[...] = jnp.zeros_like(acc)
    order = [(k, side) for k in range(4) for side in range(2)]
    for t in range(4):
        tile = lax.rem(x + 4 - t, 4)
        left = []
        for k, side in order:
            u = (near2, far2)[side] if k == 2 else (near, far)[side].at[(0, 1, None, 2)[k]]
            left.append(jnp.concatenate([u[tile * 2 + h] for h in range(2)], axis=1))
        part = dot3(jnp.concatenate(left, axis=0), vs[t, :256, :], ((1,), (0,)))
        s = plan[INFO + 5 + t]
        for i, (k, side) in enumerate(order):
            block = lax.rem(zh + 4 - k, 4) * 2 + (core if side == 0 else 1 - core)
            acc[s, block] += part[i * 64:(i + 1) * 64, :]
    diag = []
    for s in range(2):
        total = None
        for t in range(4):
            term = jnp.where(plan[INFO + 5 + t] == s, vs[t, 256:264, :], 0.0)
            total = term if total is None else total + term
        diag.append(total)
    for k in range(4):
        for zrel in range(2):
            m = ms[k * 2 + zrel]
            for s in range(2):
                m[s * 64:(s + 1) * 64, :] = acc[s, 2 * lax.rem(y + k, 4) + (zl ^ zrel)]
                m[128 + s * 8:136 + s * 8, :] = diag[s]


def prod_call(plan, vs, pieces):
    spec = pl.BlockSpec(memory_space=VMEM)
    return pl.pallas_call(
        prod_kernel,
        in_specs=[pl.BlockSpec(memory_space=SMEM)] + [spec] * 5,
        out_specs=[spec] * 8,
        out_shape=[jax.ShapeDtypeStruct((144, 256), F32)] * 8,
        scratch_shapes=[VMEM((2, 8, 64, 256), F32)],
        compiler_params=pltpu.CompilerParams(vmem_limit_bytes=24 * 2**20),
        cost_estimate=pl.CostEstimate(flops=3 * 2 * 512 * 1024 * 256, bytes_accessed=5 * 2**20,
                                      transcendentals=0),
        name="product",
    )(plan, *vs, *pieces)


def cross_kernel(plan, v, block, cross, base):
    flip = plan[INFO + 11]
    eye = lax.broadcasted_iota(jnp.int32, (256, 256), 0) == lax.broadcasted_iota(
        jnp.int32, (256, 256), 1)
    g_diag = jnp.sum(jnp.where(eye, block[...], 0.0), axis=1, keepdims=True)
    for f in range(2):
        vf = v[f ^ flip]
        cross[f] = -vf
        base[f] = g_diag + 2.0 * vf


def cross_call(plan, v, ginv):
    full = pl.BlockSpec((2, 256, 256), lambda _, plan: (0, 0, 0))
    return pl.pallas_call(
        cross_kernel,
        grid_spec=pltpu.PrefetchScalarGridSpec(
            num_scalar_prefetch=1, grid=(1,),
            in_specs=[full, pl.BlockSpec((256, 256), lambda _, plan: (0, plan[INFO + 12]))],
            out_specs=[full, full],
        ),
        out_shape=[jax.ShapeDtypeStruct((2, 256, 256), F32)] * 2,
        compiler_params=pltpu.CompilerParams(vmem_limit_bytes=12 * 2**20),
        name="cross",
    )(plan, v, ginv)


def last_kernel(plan, dinv, base, *refs):
    *ms, resist, sigma, total = refs
    sums = [ms[i][...] + ms[i + 1][...] for i in range(0, 8, 2)]
    total[...] = (sums[0] + sums[1]) + (sums[2] + sums[3])
    flip = plan[INFO + 11]
    rows = lax.broadcasted_iota(jnp.int32, (256, 256), 0)
    at = lax.broadcasted_iota(jnp.int32, (64, 256), 0) + lax.rem(plan[INFO + 12], 4) * 64
    on_diag = at == lax.broadcasted_iota(jnp.int32, (64, 256), 1)
    on_diag = on_diag & (plan[INFO + 12] // 4 == plan[INFO + 3] * 2 + plan[INFO + 4])
    for f in range(2):
        s = f ^ flip
        d = dinv[pl.ds(s, 1), :]
        sigma[:, f, :] = total[pl.ds(pl.multiple_of(s * 64, 64), 64), :] + jnp.where(on_diag, d, 0.0)
        deep = pl.ds(pl.multiple_of(128 + s * 8, 8), 8)
        diag = total[deep, :][0:1, :] + d
        live = jnp.where(plan[INFO + 9] == f, plan[INFO + 10], 0)
        resist[f] = jnp.where(rows < live, diag + base[f], 0.0)


def last_call(plan, dinv, base, ms):
    spec = pl.BlockSpec(memory_space=VMEM)
    return pl.pallas_call(
        last_kernel,
        in_specs=[pl.BlockSpec(memory_space=SMEM)] + [spec] * 10,
        out_specs=[spec] * 2,
        scratch_shapes=[VMEM((144, 256), F32)],
        out_shape=[jax.ShapeDtypeStruct((2, 256, 256), F32), jax.ShapeDtypeStruct((64, 2, 256), F32)],
        compiler_params=pltpu.CompilerParams(vmem_limit_bytes=12 * 2**20),
        name="last",
    )(plan, dinv, base, *ms)


def body(ginv, ufactor, dinv, tile_map, counts, assign):
    pin = lax.optimization_barrier

    a0 = ufactor
    b0 = send_pair(a0)
    plan = plan_call(tile_map, counts, assign)
    a1, a2, a3 = send_pq(a0, 1, 0), send_pq(a0, 2, 0), send_pq(a0, -1, 0)
    b1, b3 = send_pq(b0, 1, 0), send_pq(b0, -1, 0)
    a1, a2, a3, b0, b1, b3 = pin((a1, a2, a3, b0, b1, b3))
    ga = jnp.stack([a0, a1, a2, a3])
    ga1 = send_pq(ga, 0, 1)
    ga3 = send_pq(ga, 0, -1)
    b2, plan = pin((send_pair(a2), plan))
    gb = jnp.stack([b0, b1, b2, b3])
    gb1 = send_pq(gb[:3], 0, 1)
    gb3 = send_pq(gb[1:], 0, -1)
    carry = v_call(ginv, plan, [ga], [0], None)
    ga1, ga3, carry = pin((ga1, ga3, carry))
    ga2a = send_pq(ga1[:2], 0, 1)
    ga2b = send_pq(ga3[2:], 0, -1)
    gbr = send_pair(jnp.concatenate([ga1[3:], ga3[:1]]))
    carry = v_call(ginv, plan, [gb, ga1, ga3], [16, 4, 12], carry)
    gb1, gb3, carry = pin((gb1, gb3, carry))
    gb2a = send_pq(gb1[:2], 0, 1)
    gb2b = send_pq(gb3[1:], 0, -1)
    carry = v_call(ginv, plan, [gb1, gb3], [20, 29], carry)
    ga2a, ga2b, gbr, carry = pin((ga2a, ga2b, gbr, carry))
    gbr1, gbr3 = gbr[:1], gbr[1:]
    rows = u_call(plan, [ga, gb, ga1, ga3, gb1, gbr1, gbr3, gb3, ga2a, ga2b],
                  [0, 16, 4, 12, 20, 23, 28, 29, 8, 10], None)
    gb2a, gb2b, carry, rows = pin((gb2a, gb2b, carry, rows))
    own, ut = u_call(plan, [gb2a, gb2b], [24, 26], rows)

    c1, c3 = send_zh(ut, 1), send_zh(ut, -1)
    v, msg = v_call(ginv, plan, [ga2a, ga2b, gbr1, gbr3, gb2a, gb2b], [8, 10, 23, 28, 24, 26],
                    carry, own)
    v1, v3 = send_x(msg, 1), send_x(msg, -1)
    v2 = jnp.concatenate([send_x(v1[:136], 1), send_x(v3[136:], -1)])
    vs = jnp.stack([msg, v1, v2, v3])
    c1, c3, ut, _ = pin((c1, c3, ut, msg))
    c2 = jnp.concatenate([send_zh(c1[:4], 1), send_zh(c3[4:], -1)])
    near = [jnp.stack([ut, c1, c3]), c2]
    far = [send_core(t) for t in near]
    cross, base = cross_call(plan, v, ginv)

    m = prod_call(plan, [vs], near + far)
    r = [m[0]] + [send_yz(m[k * 2 + dz], k, dz)
                for k, dz in ((2, 1), (0, 1), (2, 0), (1, 1), (1, 0), (3, 1), (3, 0))]
    resist, sigma = last_call(plan, dinv, base, r)
    return cross, resist, sigma


def solution(mesh):
    in_specs = (P("cube", None), P(None, "cube", "col"), P(None, "col"), P(), P(), P())
    out_specs = (P(None, "cube", "col"), P(None, "cube", "col"), P("cube", None, "col"))
    return jax.shard_map(body, mesh=mesh, in_specs=in_specs, out_specs=out_specs, check_vma=False)
```
